256 devices in a mesh: dom: 64 (over z, y, x_hi), edge: 4 (over x_lo, core).
Axes of the slice: x: 4 (x_hi: 2, x_lo: 2; x = x_hi * 2 + x_lo), y: 4, z: 8, core: 2. Of those that a mesh axis runs over, the one named last changes fastest.
Arguments:
- coordinates: bfloat16 [3, 32768], P(None, 'dom'), may hold values from 0 to 1
- features: bfloat16 [32768, 128], P('dom'), may hold values from -6 to 6
- species: int32 [32768], P('dom'), may hold values from 0 to 88
- ghost_map: int32 [1664, 64], P('dom'), may hold values from 0 to 511
- edge_sender: int32 [2097152], P(('dom', 'edge')), may hold values from 0 to 2175
- edge_receiver: int32 [2097152], P(('dom', 'edge')), may hold values from 0 to 511, as said below
- edge_count: int32 [64], P('dom'), may hold values from 16384 to 32768, as said below
- w_up: bfloat16 [128, 128], replicated, may hold values from -0.5 to 0.5
- radial_one: float32 [8, 64], replicated, may hold values from -2 to 2
- radial_two: float32 [64, 64], replicated, may hold values from -0.75 to 0.75
- radial_three: float32 [64, 384], replicated, may hold values from -0.75 to 0.75
- read_mix: float32 [640, 128], replicated, may hold values from -0.25 to 0.25
- species_out: float32 [89, 128], replicated, may hold values from -0.5 to 0.5
Outputs:
- energies: float32 [32768], P(('dom', 'edge'))
- forces: float32 [3, 32768], P(None, ('dom', 'edge'))
- feature_grad: float32 [32768, 128], P(('dom', 'edge'))
The draws below stay inside these ranges and needn't reach their ends.
Inputs may be any that keep to these rules, and one draw needn't show every extreme that they name: The valid edge slots of a subdomain are its first edge_count slots; in every draw some subdomain uses all 32768. `edge_receiver`: within each subdomain's 32768 slots every owned atom is the receiver of exactly 64 slots, in no particular order.
All inputs are finite; a program needn't handle non-finite values.
Results may differ from the reference program's by a relative error of at most 0.0029.
Values may be sent and summed in bfloat16 or wider, within the bound.
A program may use at most 128 MiB of HBM per device.

```python
import math
import jax
import jax.numpy as jnp
import numpy as np
from jax import lax

CHANNELS = 128
RADIAL = 64
BASIS = 8
ELEMENTS = 89
ATOMS_DEV = 512
SLOTS_ATOM = 64
GHOST_SLOT = 64
EDGES = 32768
NATOMS = 32768
GHOSTS = 1664
N_DOM = 64


def draw_edge_count(key, part):
    key = jax.random.fold_in(key, 5)
    key_counts, key_full = jax.random.split(key)
    counts = jax.random.randint(key_counts, (N_DOM,), EDGES // 2, EDGES + 1)
    full_at = jax.random.randint(key_full, (), 0, N_DOM)
    return jnp.where(jnp.arange(N_DOM) == full_at, EDGES, counts).astype(jnp.int32)


def draw_edge_receiver(key, part):
    key = jax.random.fold_in(key, 11)
    domain_keys = jax.random.split(key, N_DOM)
    base_list = (jnp.arange(EDGES, dtype=jnp.int32) // SLOTS_ATOM).astype(jnp.int32)

    def one_list(domain_key):
        return jax.random.permutation(domain_key, base_list)
    return jax.vmap(one_list)(domain_keys).reshape(-1).astype(jnp.int32)


def with_ends(drawn, own_key, smallest, largest):
    longest = drawn.shape.index(max(drawn.shape))
    spots = []
    for shift in (0, 1):
        where = [jax.random.randint(jax.random.fold_in(own_key, axis), (), 0, length) for axis, length in enumerate(drawn.shape)]
        where[longest] = (where[longest] + shift) % drawn.shape[longest]
        spots.append(tuple(where))
    return drawn.at[spots[0]].set(smallest).at[spots[1]].set(largest)


def levels(key, extent, pieces, smallest, top_value):
    factor_of, own = 1.0, jax.random.fold_in(key, 6)
    for dim, blocks in pieces:
        steps = jnp.exp(jax.random.uniform(jax.random.fold_in(own, dim), (blocks,), jnp.float32, smallest / len(pieces), top_value / len(pieces)))
        factor_of = factor_of * jnp.repeat(steps, extent[dim] // blocks).reshape([-1 if axis == dim else 1 for axis in range(len(extent))])
    return factor_of


def rank_table(count, skew):
    portions = [(1 << 20) // math.isqrt(standing ** skew) + 1 for standing in range(1, count + 1)]
    scale = 1 + sum(portions) // (1 << 30)
    return np.cumsum(np.array([max(1, weight // scale) for weight in portions]))


def ranked(rng, shape, count, skew):
    listing = rank_table(count, skew)
    lot = jax.random.randint(jax.random.fold_in(rng, 1), shape, 0, int(listing[count - 1]))
    standing = jnp.searchsorted(jnp.asarray(listing, jnp.int32), lot, side="right")
    return jax.random.permutation(jax.random.fold_in(rng, 2), count)[standing].astype(jnp.int32)


def centred(stream_key, dims, scale, bound, shards=(), kind=jnp.bfloat16):
    entries = scale * jax.random.normal(stream_key, dims, jnp.float32)
    if shards:
        entries = entries * levels(stream_key, dims, shards, -0.22, 0.18)
    return jnp.clip(entries, -bound, bound).astype(kind)


def setup_inputs(seed: int = 0) -> dict:
    key_list = jax.random.split(jax.random.key(seed), 14)
    coordinates = jnp.clip(1.0 * jax.random.uniform(key_list[0], (3, NATOMS), jnp.float32) ** levels(key_list[0], (3, NATOMS), ((1, 64),), -0.2, 0.2), 0.0, 1.0).astype(jnp.bfloat16)
    features = centred(key_list[1], (NATOMS, CHANNELS), 1.0, 6.0, ((0, 64),))
    species = with_ends(ranked(key_list[2], (NATOMS,), ELEMENTS, 2), jax.random.fold_in(key_list[2], 3), 0, ELEMENTS - 1).astype(jnp.int32)
    ghost_map = with_ends(jax.random.randint(key_list[3], (N_DOM * 26, GHOST_SLOT), 0, ATOMS_DEV), jax.random.fold_in(key_list[3], 1), 0, ATOMS_DEV - 1).astype(jnp.int32)
    edge_sender = with_ends(jax.random.randint(key_list[4], (N_DOM * EDGES,), 0, ATOMS_DEV + GHOSTS), jax.random.fold_in(key_list[4], 1), 0, (ATOMS_DEV + GHOSTS) - 1).astype(jnp.int32)
    edge_receiver = draw_edge_receiver(jax.random.fold_in(key_list[13], 71), 0)
    edge_count = draw_edge_count(jax.random.fold_in(key_list[13], 71), 0)
    w_up = centred(key_list[7], (CHANNELS, CHANNELS), CHANNELS ** -0.5, 0.5)
    radial_one = centred(key_list[8], (BASIS, RADIAL), BASIS ** -0.5, 2.0, (), jnp.float32)
    radial_two = centred(key_list[9], (RADIAL, RADIAL), RADIAL ** -0.5, 0.75, (), jnp.float32)
    radial_three = centred(key_list[10], (RADIAL, 3 * CHANNELS), RADIAL ** -0.5, 0.75, (), jnp.float32)
    read_mix = centred(key_list[11], (5 * CHANNELS, CHANNELS), (5 * CHANNELS) ** -0.5, 0.25, (), jnp.float32)
    species_out = centred(key_list[12], (ELEMENTS, CHANNELS), CHANNELS ** -0.5, 0.5, (), jnp.float32)
    return {"coordinates": coordinates, "features": features, "species": species, "ghost_map": ghost_map, "edge_sender": edge_sender, "edge_receiver": edge_receiver, "edge_count": edge_count, "w_up": w_up, "radial_one": radial_one, "radial_two": radial_two, "radial_three": radial_three, "read_mix": read_mix, "species_out": species_out}


HIGH = lax.Precision.HIGHEST

def cube_side(device_count):
    grid_side = 1
    while grid_side * grid_side * grid_side < device_count:
        grid_side = grid_side + 1
    return grid_side

def offset_table():
    return [(first_axis, second_axis, third_axis) for first_axis in (-1, 0, 1) for second_axis in (-1, 0, 1) for third_axis in (-1, 0, 1) if (first_axis, second_axis, third_axis) != (0, 0, 0)]

def radial_part(squared, edge_valid, radial_one, radial_two, radial_three):
    basis_count = radial_one.shape[0]
    betas = 0.4 * 15.0 ** (jnp.arange(basis_count, dtype=jnp.float32) / (basis_count - 1))
    basis = jnp.exp(-squared[:, None] * betas[None, :])
    envelope = jnp.square(jnp.maximum(0.0, 1.0 - squared / 4.0)) * edge_valid
    hidden_one = jax.nn.silu(jnp.dot(basis, radial_one, precision=HIGH))
    hidden_two = jax.nn.silu(jnp.dot(hidden_one, radial_two, precision=HIGH))
    return jnp.dot(hidden_two, radial_three, precision=HIGH) * envelope[:, None]

def harmonics(relative, squared):
    along_x = relative[0]
    along_y = relative[1]
    along_z = relative[2]
    return jnp.stack([jnp.ones_like(squared), along_x, along_y, along_z, along_x * along_y, along_y * along_z, along_x * along_z, along_x * along_x - squared / 3.0, along_y * along_y - squared / 3.0], axis=1)

def block_messages(positions, features_all, senders, receivers, edge_valid, weights):
    pos_send = jnp.take(positions, senders, axis=1)
    pos_recv = jnp.take(positions, receivers, axis=1)
    relative = pos_send - pos_recv
    squared = lax.optimization_barrier(jnp.sum(relative * relative, axis=0))
    radial = radial_part(squared, edge_valid, weights[0], weights[1], weights[2])
    channels = features_all.shape[1]
    degree_terms = radial.reshape(-1, 3, channels) * jnp.take(features_all, senders, axis=0)[:, None, :]
    spread = jnp.concatenate([degree_terms[:, 0:1], jnp.repeat(degree_terms[:, 1:2], 3, axis=1), jnp.repeat(degree_terms[:, 2:3], 5, axis=1)], axis=1)
    message = spread * harmonics(relative, squared)[:, :, None]
    return message.reshape(-1, 9 * channels)

def edge_sums(positions, features_all, senders, receivers, edge_valid, weights, atom_count):
    edge_total = senders.shape[0]
    block_size = min(1024, edge_total)
    block_count = edge_total // block_size

    def step_block(accum, items):
        send_rows, recv_rows, keep_rows = items
        message = block_messages(positions, features_all, send_rows, recv_rows, keep_rows, weights)
        return (accum + jax.ops.segment_sum(message, recv_rows, num_segments=atom_count), None)
    initial = jnp.zeros((atom_count, 9 * features_all.shape[1]), jnp.float32)
    accum, _ = lax.scan(jax.checkpoint(step_block), initial, (senders.reshape(block_count, block_size), receivers.reshape(block_count, block_size), edge_valid.reshape(block_count, block_size)))
    return accum * (1.0 / math.sqrt(SLOTS_ATOM))

def readout(node_data, kinds, read_mix, species_out):
    channels = species_out.shape[1]
    blocks = node_data.reshape(-1, 9, channels)
    scalar = blocks[:, 0]
    vector_x = blocks[:, 1]
    vector_y = blocks[:, 2]
    vector_z = blocks[:, 3]
    comp_xy = blocks[:, 4]
    comp_yz = blocks[:, 5]
    comp_xz = blocks[:, 6]
    comp_xx = blocks[:, 7]
    comp_yy = blocks[:, 8]
    comp_zz = -comp_xx - comp_yy
    norm_one = vector_x * vector_x + vector_y * vector_y + vector_z * vector_z
    norm_two = comp_xx * comp_xx + comp_yy * comp_yy + comp_zz * comp_zz + 2.0 * (comp_xy * comp_xy + comp_yz * comp_yz + comp_xz * comp_xz)
    cubic_term = comp_xx * vector_x * vector_x + comp_yy * vector_y * vector_y + comp_zz * vector_z * vector_z + 2.0 * (comp_xy * vector_x * vector_y + comp_yz * vector_y * vector_z + comp_xz * vector_x * vector_z)
    invariants = jnp.concatenate([scalar, norm_one, norm_two, scalar * norm_one, cubic_term], axis=1)
    hidden = jax.nn.silu(jnp.dot(invariants, read_mix, precision=HIGH))
    onehot = (kinds[:, None] == jnp.arange(species_out.shape[0], dtype=jnp.int32)[None, :]).astype(jnp.float32)
    per_kind = jnp.dot(onehot, species_out, precision=HIGH)
    return lax.optimization_barrier(jnp.sum(hidden * per_kind, axis=1))

def reference(coordinates, features, species, ghost_map, edge_sender, edge_receiver, edge_count, w_up, radial_one, radial_two, radial_three, read_mix, species_out):
    grid_side = cube_side(N_DOM)
    offsets = offset_table()
    shift_values = jnp.array([offset[0] * grid_side * grid_side + offset[1] * grid_side + offset[2] for offset in offsets], dtype=jnp.int32)
    offset_array = jnp.array(offsets, dtype=jnp.float32)
    hprime = jnp.dot(features, w_up, preferred_element_type=jnp.float32).astype(jnp.bfloat16)
    hprime_wide = lax.optimization_barrier(hprime).astype(jnp.float32)
    coords_wide = coordinates.astype(jnp.float32)
    map_table = ghost_map.reshape(N_DOM, 26, GHOST_SLOT)
    weights = (radial_one, radial_two, radial_three)

    def one_domain(domain):
        sources = jnp.mod(domain - shift_values, N_DOM).astype(jnp.int32)
        picked = map_table[sources, jnp.arange(26, dtype=jnp.int32)]
        global_index = (sources[:, None] * ATOMS_DEV + picked).reshape(-1).astype(jnp.int32)
        atom_start = (domain * ATOMS_DEV).astype(jnp.int32)
        edge_start = (domain * EDGES).astype(jnp.int32)
        ghost_coords = jnp.take(coords_wide, global_index, axis=1).reshape(3, 26, GHOST_SLOT) - offset_array.T[:, :, None]
        own_coords = lax.dynamic_slice_in_dim(coords_wide, atom_start, ATOMS_DEV, axis=1)
        pos_all = jnp.concatenate([own_coords, ghost_coords.reshape(3, -1)], axis=1)
        own_rows = lax.dynamic_slice_in_dim(hprime_wide, atom_start, ATOMS_DEV, axis=0)
        h_all = jnp.concatenate([own_rows, jnp.take(hprime_wide, global_index, axis=0)], axis=0)
        edge_valid = (jnp.arange(EDGES, dtype=jnp.int32) < edge_count[domain]).astype(jnp.float32)
        senders = lax.dynamic_slice_in_dim(edge_sender, edge_start, EDGES)
        receivers = lax.dynamic_slice_in_dim(edge_receiver, edge_start, EDGES)
        kinds = lax.dynamic_slice_in_dim(species, atom_start, ATOMS_DEV)

        def energy_of(positions, row_data):
            sums = edge_sums(positions, row_data, senders, receivers, edge_valid, weights, ATOMS_DEV)
            return readout(sums, kinds, read_mix, species_out)
        energy, pull_back = jax.vjp(energy_of, pos_all, h_all)
        pos_grad, row_grad = pull_back(jnp.ones_like(energy))
        return (energy, pos_grad, row_grad, global_index)
    energy_all, pos_grads, row_grads, index_all = lax.map(one_domain, jnp.arange(N_DOM, dtype=jnp.int32))
    energies = energy_all.reshape(NATOMS)
    flat_index = index_all.reshape(-1)
    own_pos = pos_grads[:, :, :ATOMS_DEV].transpose(1, 0, 2).reshape(3, NATOMS)
    ghost_pos = pos_grads[:, :, ATOMS_DEV:].transpose(1, 0, 2).reshape(3, -1)
    total_pos = own_pos.at[:, flat_index].add(ghost_pos)
    own_rows_grad = row_grads[:, :ATOMS_DEV].reshape(NATOMS, CHANNELS)
    ghost_rows_grad = row_grads[:, ATOMS_DEV:].reshape(-1, CHANNELS)
    total_rows = own_rows_grad.at[flat_index].add(ghost_rows_grad)
    forces = -total_pos
    feature_grad = jnp.dot(total_rows, w_up.astype(jnp.float32).T, precision=HIGH)
    return (energies, forces, feature_grad)
```

```python
import jax
import jax.numpy as jnp
from jax import lax
from jax.experimental import pallas as pl
from jax.experimental.pallas import tpu as pltpu
from jax.sharding import PartitionSpec as P

F32, BF16, I32 = jnp.float32, jnp.bfloat16, jnp.int32
HIGH = lax.Precision.HIGHEST
MESH = pl.DeviceIdType.MESH
VMEM_SPEC = pl.BlockSpec(memory_space=pltpu.VMEM)

CH = 128
ATOMS = 512
OWN = 128
RANKS = 64
SLOT = 64
NOFF = 26
PAIRS = NOFF // 2
QUART = 4
EDGE_ROWS = 64
GROUPS = 9
GROWS = 144
NE = 256
STEPS = OWN * RANKS // NE
BLK = 80
SENTINEL = 4095
LIMIT = 56 * 1024 * 1024

OFFSETS = [
    (a, b, c)
    for a in (-1, 0, 1)
    for b in (-1, 0, 1)
    for c in (-1, 0, 1)
    if (a, b, c) != (0, 0, 0)
]


def shifts(count):
    side = 1
    while side * side * side < count:
        side += 1
    return [o[0] * side * side + o[1] * side + o[2] for o in OFFSETS]


def mm(a, b):
    return lax.dot_general(a, b, (((1,), (0,)), ((), ())), preferred_element_type=F32)


def mm_nt(a, b):
    return lax.dot_general(a, b, (((1,), (1,)), ((), ())), preferred_element_type=F32)


def mm_high(a, b):
    return lax.dot_general(
        a, b, (((1,), (0,)), ((), ())), precision=HIGH, preferred_element_type=F32
    )


def split(x):
    hi = x.astype(BF16)
    return hi, (x - hi.astype(F32)).astype(BF16)


def weight_stack(w):
    hi, lo = split(w)
    return jnp.concatenate([hi, hi, lo], axis=1)


def value_stack(x):
    hi, lo = split(x)
    return jnp.concatenate([hi, lo, hi], axis=0)


def iota(shape, dim):
    return lax.broadcasted_iota(I32, shape, dim)


def pair_rows(gmap_ref, p):
    return jnp.concatenate([gmap_ref[2 * p : 2 * p + 1, :], gmap_ref[2 * p + 1 : 2 * p + 2, :]], axis=1)


def neighbours(dom_size, number, sign):
    me = lax.axis_index("dom")
    step = shifts(dom_size)[number] * sign
    return lax.rem(me + (step % dom_size), dom_size)


def greet(dom_size):
    barrier = pltpu.get_barrier_semaphore()
    quarter = lax.axis_index("edge")
    me = lax.axis_index("dom")
    for number in range(NOFF):
        there = neighbours(dom_size, number, 1)
        pl.semaphore_signal(barrier, inc=1, device_id=(there, quarter), device_id_type=MESH)
    for j in range(1, QUART):
        peer = lax.rem(quarter + j, QUART)
        pl.semaphore_signal(barrier, inc=1, device_id=(me, peer), device_id_type=MESH)
    return barrier


def exchange_kernel(
    dom_size,
    feat_ref, wup_ref, coord_ref, gmap_ref, snd_ref, rcv_ref, cnt_ref,
    slots_ref, blocks_ref, own_ref,
    sendblk, epack, li_s, g_s, hi_s, tri_s, send_sem, recv_sem,
):
    me = lax.axis_index("dom")
    quarter = lax.axis_index("edge")
    barrier = greet(dom_size)

    first = quarter * (EDGE_ROWS * 128)
    index = first + iota((EDGE_ROWS, 128), 0) * 128 + iota((EDGE_ROWS, 128), 1)
    sender = jnp.where(index < cnt_ref[0], snd_ref[...], SENTINEL)
    epack[quarter] = sender + rcv_ref[...] * 65536

    hprime = mm(feat_ref[...], wup_ref[...]).astype(BF16)
    h_t = hprime.astype(F32).T.astype(BF16)
    own_ref[...] = h_t
    coords = jnp.concatenate(
        [coord_ref[...].astype(F32), jnp.zeros((13, ATOMS), F32)], axis=0
    ).astype(BF16)
    ext = jnp.concatenate([h_t, coords], axis=0)

    pl.semaphore_wait(barrier, NOFF + QUART - 1)

    copies = []
    for j in range(1, QUART):
        peer = lax.rem(quarter + j, QUART)
        copy = pltpu.make_async_remote_copy(
            src_ref=epack.at[quarter],
            dst_ref=epack.at[quarter],
            send_sem=send_sem.at[NOFF + j - 1],
            recv_sem=recv_sem.at[NOFF + j - 1],
            device_id=(me, peer),
            device_id_type=MESH,
        )
        copy.start()
        copies.append(copy)

    low = iota((64, 128), 1) < 64
    low16 = iota((16, 128), 1) < 64
    ghosts = []
    for p in range(PAIRS):
        row = pair_rows(gmap_ref, p)
        onehot = jnp.where(iota((ATOMS, 128), 0) == row, 1.0, 0.0).astype(BF16)
        picked = mm(ext, onehot)
        top, bottom, pos = picked[0:64], picked[64:128], picked[128:144]
        even = jnp.where(low, top, pltpu.roll(bottom, 64, 1))
        odd = jnp.where(low, pltpu.roll(top, 64, 1), bottom)
        sendblk[2 * p, 0:64, :] = even.astype(BF16)
        sendblk[2 * p + 1, 0:64, :] = odd.astype(BF16)
        sendblk[2 * p, 64:80, :] = jnp.where(low16, pos, 0.0).astype(BF16)
        sendblk[2 * p + 1, 64:80, :] = jnp.where(low16, pltpu.roll(pos, 64, 1), 0.0).astype(BF16)
        for number in (2 * p, 2 * p + 1):
            copy = pltpu.make_async_remote_copy(
                src_ref=sendblk.at[number],
                dst_ref=blocks_ref.at[number],
                send_sem=send_sem.at[number],
                recv_sem=recv_sem.at[number],
                device_id=(neighbours(dom_size, number, 1), quarter),
                device_id_type=MESH,
            )
            copy.start()
            ghosts.append(copy)

    for copy in copies:
        copy.wait_recv()

    packed = epack[...].reshape(QUART * EDGE_ROWS, 128)
    local = (packed >> 16) - quarter * OWN
    inside = (local >= 0) & (local < OWN)
    li_s[...] = jnp.where(inside, local, 255).astype(F32)
    value = packed & 65535
    g_s[...] = (value >> 8).astype(F32)
    hi_s[...] = (value & 255).astype(F32)
    tri_s[:, 0:256] = jnp.where(iota((256, 256), 0) < iota((256, 256), 1), 1.0, 0.0).astype(BF16)
    tri_s[:, 256:384] = jnp.ones((256, 128), BF16)

    atom = iota((OWN, 256), 0).astype(F32)
    rank_of = iota((RANKS, 256), 0).astype(F32)

    def sort_step(step, carry):
        base, total = carry
        rows = pl.ds(pl.multiple_of(step * 8, 8), 8)
        li8, g8, hi8 = li_s[rows, :], g_s[rows, :], hi_s[rows, :]

        def lane_row(x, b):
            return jnp.concatenate([x[2 * b : 2 * b + 1], x[2 * b + 1 : 2 * b + 2]], axis=1)

        hots = [jnp.where(atom == lane_row(li8, b), 1.0, 0.0) for b in range(4)]
        hots16 = [hot.astype(BF16) for hot in hots]
        counts = mm(jnp.concatenate(hots16, axis=0), tri_s[...])
        lefts = []
        for b in range(4):
            block = counts[OWN * b : OWN * (b + 1)]
            before = block[:, 0:256] + jnp.concatenate([base, base], axis=1)
            base = base + block[:, 256:384]
            rank = jnp.sum(before * hots[b], axis=0, keepdims=True)
            here = rank_of == rank
            lefts.append(
                jnp.concatenate(
                    [
                        jnp.where(here, lane_row(g8, b), 0.0).astype(BF16),
                        jnp.where(here, lane_row(hi8, b), 0.0).astype(BF16),
                    ],
                    axis=0,
                )
            )
        total = total + mm_nt(jnp.concatenate(lefts, axis=1), jnp.concatenate(hots16, axis=1))
        return base, total

    zero = jnp.zeros((OWN, 128), F32)
    _, total = lax.fori_loop(0, QUART * EDGE_ROWS // 8, sort_step, (zero, zero))
    slots_ref[...] = (total[0:64] * 256.0 + total[64:128]).astype(I32)

    for copy in ghosts:
        copy.wait_recv()
    for copy in copies + ghosts:
        copy.wait_send()


def compute_kernel(
    slots_ref, blocks_ref, own_ref, coord_ref, species_ref,
    w1_ref, w2_ref, w3_ref, mix_ref, sp_ref,
    energy_ref, gblocks_ref, gown_ref,
    tab, hot_s, acc, rad_s, h_s, d1_s, d2_s, bas_s, row_s, scat, sp_s,
    w1f, w2f, w3f, w1b, w2b, w3b, myc,
):
    quarter = lax.axis_index("edge")
    lane = iota((64, 128), 1)
    low = lane < 64
    low8 = iota((8, 128), 1) < 64
    low16 = iota((16, 128), 1) < 64
    sub8 = iota((8, 128), 0)

    coords = coord_ref[...].astype(F32)
    coords16 = jnp.concatenate([coords, jnp.zeros((13, ATOMS), F32)], axis=0).astype(BF16)
    for g in range(2):
        tab[GROWS * g : GROWS * g + 128, :] = own_ref[:, 256 * g : 256 * g + 256]
        tab[GROWS * g + 128 : GROWS * (g + 1), :] = coords16[:, 256 * g : 256 * g + 256]
    tab[GROWS * 8 : GROWS * 9, :] = jnp.zeros((GROWS, 256), BF16)
    for p in range(PAIRS):
        g, at = 2 + p // 2, 128 * (p % 2)
        even = blocks_ref[2 * p].astype(F32)
        odd = blocks_ref[2 * p + 1].astype(F32)
        top = jnp.where(low, even[0:64], pltpu.roll(odd[0:64], 64, 1))
        bottom = jnp.where(low, pltpu.roll(even[0:64], 64, 1), odd[0:64])
        pos = jnp.where(low16, even[64:80], pltpu.roll(odd[64:80], 64, 1))
        oe, oo = OFFSETS[2 * p], OFFSETS[2 * p + 1]
        off = jnp.zeros((16, 128), F32)
        sub16 = iota((16, 128), 0)
        for c in range(3):
            if oe[c] != 0 or oo[c] != 0:
                off = jnp.where(sub16 == 3 + c, jnp.where(low16, float(oe[c]), float(oo[c])), off)
        pos = pos + off
        tab[GROWS * g : GROWS * g + 64, at : at + 128] = top.astype(BF16)
        tab[GROWS * g + 64 : GROWS * g + 128, at : at + 128] = bottom.astype(BF16)
        tab[GROWS * g + 128 : GROWS * (g + 1), at : at + 128] = pos.astype(BF16)

    w1f[...] = weight_stack(w1_ref[...].T)
    w2f[...] = weight_stack(w2_ref[...].T)
    w3f[...] = weight_stack(w3_ref[...].T)
    w1b[...] = weight_stack(w1_ref[...])
    w2b[...] = weight_stack(w2_ref[...])
    hi, lo = split(w3_ref[...])
    w3b[...] = jnp.concatenate([hi, lo], axis=0)

    acc[...] = jnp.zeros(acc.shape, F32)
    scat[...] = jnp.zeros(scat.shape, F32)
    mine = pl.ds(pl.multiple_of(quarter * OWN, OWN), OWN)
    my_coords = coord_ref[:, mine].astype(F32)
    for c in range(3):
        mc = jnp.broadcast_to(my_coords[c : c + 1], (8, 128))
        myc[8 * c : 8 * c + 8, :] = jnp.concatenate([mc, mc], axis=1)

    beta = jnp.zeros((8, NE), F32)
    for n in range(8):
        beta = jnp.where(iota((8, NE), 0) == n, 0.4 * 15.0 ** (n / 7.0), beta)

    def slot_row(step):
        s = jnp.concatenate(
            [slots_ref[pl.ds(2 * step, 1), :], slots_ref[pl.ds(2 * step + 1, 1), :]], axis=1
        )
        return jnp.broadcast_to(s, (8, NE))

    def harmonic(x, y, z, dsq):
        third = dsq * (1.0 / 3.0)
        return [None, x, y, z, x * y, y * z, x * z, x * x - third, y * y - third]

    degree = [0, 1, 1, 1, 2, 2, 2, 2, 2]

    def fwd(step, carry):
        lanes = pl.ds(pl.multiple_of(step * NE, NE), NE)
        s = slot_row(step)
        group = s >> 8
        hi = s & 255
        valid = jnp.where(group < GROUPS, 1.0, 0.0)
        sub = iota((8, NE), 0)
        onehot = jnp.concatenate(
            [jnp.where(sub + 8 * t == hi, 1.0, 0.0) for t in range(32)], axis=0
        ).astype(BF16)
        hot_s[:, lanes] = onehot
        got = mm(tab[...], onehot)
        masks = [group == k for k in range(GROUPS)]
        rows = []
        for t in range(17):
            v = jnp.zeros((8, NE), F32)
            for k in range(GROUPS):
                at = GROWS * k + 8 * t
                v = jnp.where(masks[k], got[at : at + 8], v)
            rows.append(v)
        pos = rows[16]
        rel = []
        for c in range(3):
            sent = pos[c : c + 1] - pos[3 + c : 4 + c]
            rel.append(jnp.broadcast_to(sent, (8, NE)) - myc[8 * c : 8 * c + 8, :])
        x, y, z = rel
        dsq = x * x + y * y + z * z
        e0 = jnp.maximum(0.0, 1.0 - dsq * 0.25) * valid
        env = e0 * e0
        basis = jnp.exp(-dsq * beta)
        packed = jnp.zeros((8, NE), F32)
        for j, v in enumerate((x, y, z, dsq, env, e0)):
            packed = jnp.where(sub == j, v, packed)
        row_s[:, lanes] = packed
        bas_s[:, lanes] = basis

        def act(pre):
            sig = 0.5 + 0.5 * jnp.tanh(0.5 * pre)
            out = pre * sig
            return out, sig + out * (1.0 - sig)

        h1, d1 = act(mm(w1f[...], value_stack(basis)))
        d1_s[:, lanes] = d1
        h2, d2 = act(mm(w2f[...], value_stack(h1)))
        d2_s[:, lanes] = d2
        rad = mm(w3f[...], value_stack(h2))
        rad_s[:, lanes] = rad
        ys = harmonic(x, y, z, dsq)
        for t in range(16):
            h = rows[t]
            h_s[8 * t : 8 * t + 8, lanes] = h
            he = h * env
            ds = [he * rad[128 * l + 8 * t : 128 * l + 8 * t + 8] for l in range(3)]
            for m in range(9):
                msg = ds[degree[m]] if m == 0 else ds[degree[m]] * ys[m]
                at = 128 * m + 8 * t
                acc[at : at + 8, :] += msg[:, 0:128] + msg[:, 128:256]
        return carry

    lax.fori_loop(0, STEPS, fwd, 0)

    def node(m):
        return acc[128 * m : 128 * m + 128, :] * 0.125

    a0, vx, vy, vz, xy, yz, xz, xx, yy = [node(m) for m in range(9)]
    zz = -xx - yy
    n1 = vx * vx + vy * vy + vz * vz
    n2 = xx * xx + yy * yy + zz * zz + 2.0 * (xy * xy + yz * yz + xz * xz)
    cx = xx * vx + xy * vy + xz * vz
    cy = xy * vx + yy * vy + yz * vz
    cz = xz * vx + yz * vy + zz * vz
    cub = cx * vx + cy * vy + cz * vz
    inv = jnp.concatenate([a0, n1, n2, a0 * n1, cub], axis=0)
    pre = mm_high(mix_ref[...].T, inv)
    sig = 0.5 + 0.5 * jnp.tanh(0.5 * pre)
    hid = pre * sig
    sp_s[...] = jnp.zeros((128, 128), F32)
    sp_s[0:89, :] = sp_ref[...]
    kinds = species_ref[pl.ds(quarter, 1), :]
    kind_hot = jnp.where(iota((128, 128), 0) == kinds, 1.0, 0.0)
    per_kind = mm_high(sp_s[...].T, kind_hot)
    energy_ref[...] = jnp.sum(hid * per_kind, axis=0, keepdims=True)
    dpre = per_kind * (sig + hid * (1.0 - sig))
    dinv = mm_high(mix_ref[...], dpre) * 0.125
    g0, g1, g2, g3, g4 = [dinv[128 * j : 128 * j + 128] for j in range(5)]
    w = 2.0 * (g1 + g3 * a0)
    c2 = 2.0 * g4
    acc[0:128, :] = g0 + g3 * n1
    acc[128:256, :] = w * vx + c2 * cx
    acc[256:384, :] = w * vy + c2 * cy
    acc[384:512, :] = w * vz + c2 * cz
    acc[512:640, :] = 4.0 * xy * g2 + c2 * vx * vy
    acc[640:768, :] = 4.0 * yz * g2 + c2 * vy * vz
    acc[768:896, :] = 4.0 * xz * g2 + c2 * vx * vz
    acc[896:1024, :] = 2.0 * g2 * (xx - zz) + g4 * (vx * vx - vz * vz)
    acc[1024:1152, :] = 2.0 * g2 * (yy - zz) + g4 * (vy * vy - vz * vz)

    def bwd(step, down):
        lanes = pl.ds(pl.multiple_of(step * NE, NE), NE)
        group = slot_row(step) >> 8
        rows = row_s[:, lanes]
        x, y, z, dsq, env, e0 = [jnp.broadcast_to(rows[j : j + 1], (8, NE)) for j in range(6)]
        ys = harmonic(x, y, z, dsq)
        denv = jnp.zeros((8, NE), F32)
        dys = [jnp.zeros((8, NE), F32) for _ in range(9)]
        dhs, drs = [], [[], [], []]
        for t in range(16):
            da = []
            for m in range(9):
                v = acc[128 * m + 8 * t : 128 * m + 8 * t + 8, :]
                da.append(jnp.concatenate([v, v], axis=1))
            t0 = da[0]
            t1 = x * da[1] + y * da[2] + z * da[3]
            t2 = ys[4] * da[4]
            for m in range(5, 9):
                t2 = t2 + ys[m] * da[m]
            ts = [t0, t1, t2]
            rs = [rad_s[128 * l + 8 * t : 128 * l + 8 * t + 8, lanes] for l in range(3)]
            u = rs[0] * t0 + rs[1] * t1 + rs[2] * t2
            h = h_s[8 * t : 8 * t + 8, lanes]
            he = h * env
            denv = denv + h * u
            dhs.append(env * u)
            for l in range(3):
                drs[l].append(he * ts[l])
            d1, d2 = he * rs[1], he * rs[2]
            for m in range(1, 9):
                dys[m] = dys[m] + (d1 if m < 4 else d2) * da[m]

        def total(v):
            return jnp.broadcast_to(jnp.sum(v, axis=0, keepdims=True), (8, NE))

        drad = jnp.concatenate(drs[0] + drs[1] + drs[2], axis=0).astype(BF16)
        both = mm(w3b[...], drad)
        dp2 = (both[0:64] + both[64:128]) * d2_s[:, lanes]
        dp1 = mm(w2b[...], value_stack(dp2)) * d1_s[:, lanes]
        dbas = mm(w1b[...], value_stack(dp1))
        denv = total(denv)
        dys = [None] + [total(v) for v in dys[1:]]
        ddsq = (
            -total(dbas * bas_s[:, lanes] * beta)
            - 0.5 * e0 * denv
            - (dys[7] + dys[8]) * (1.0 / 3.0)
        )
        two = 2.0 * ddsq
        dx = dys[1] + y * dys[4] + z * dys[6] + 2.0 * x * dys[7] + x * two
        dy = dys[2] + x * dys[4] + z * dys[5] + 2.0 * y * dys[8] + y * two
        dz = dys[3] + y * dys[5] + x * dys[6] + z * two
        sub = iota((8, NE), 0)
        drel = jnp.where(sub == 0, dx, jnp.where(sub == 1, dy, jnp.where(sub == 2, dz, 0.0)))
        drel_hi = drel.astype(BF16).astype(F32)
        flow = jnp.concatenate(dhs + [drel_hi, drel - drel_hi], axis=0).astype(BF16)
        group16 = jnp.concatenate([group, group], axis=0)
        lefts = []
        for k in range(GROUPS):
            mask = jnp.where(group16 == k, 1.0, 0.0).astype(BF16)
            lefts.extend(flow[16 * t : 16 * t + 16] * mask for t in range(9))
        scat[...] += mm_nt(jnp.concatenate(lefts, axis=0), hot_s[:, lanes])
        return down + drel[:, 0:128] + drel[:, 128:256]

    down = lax.fori_loop(0, STEPS, bwd, jnp.zeros((8, 128), F32))

    for g in range(2):
        span = slice(256 * g, 256 * g + 256)
        gown_ref[0:128, span] = scat[GROWS * g : GROWS * g + 128, :]
        gown_ref[128:136, span] = (
            scat[GROWS * g + 128 : GROWS * g + 136, :] + scat[GROWS * g + 136 : GROWS * g + 144, :]
        )
    gown_ref[128:136, mine] = gown_ref[128:136, mine] - down
    for p in range(PAIRS):
        g, at = 2 + p // 2, 128 * (p % 2)
        top = scat[GROWS * g : GROWS * g + 64, at : at + 128]
        bottom = scat[GROWS * g + 64 : GROWS * g + 128, at : at + 128]
        pos = (
            scat[GROWS * g + 128 : GROWS * g + 136, at : at + 128]
            + scat[GROWS * g + 136 : GROWS * g + 144, at : at + 128]
        )
        pos_hi = pos.astype(BF16).astype(F32)
        pos = jnp.concatenate([pos_hi, pos - pos_hi], axis=0)
        even = jnp.where(low, top, pltpu.roll(bottom, 64, 1))
        odd = jnp.where(low, pltpu.roll(top, 64, 1), bottom)
        gblocks_ref[2 * p, 0:64, :] = even.astype(BF16)
        gblocks_ref[2 * p + 1, 0:64, :] = odd.astype(BF16)
        gblocks_ref[2 * p, 64:80, :] = jnp.where(low16, pos, 0.0).astype(BF16)
        gblocks_ref[2 * p + 1, 64:80, :] = jnp.where(low16, pltpu.roll(pos, 64, 1), 0.0).astype(BF16)


def return_kernel(
    dom_size,
    gblocks_ref, gown_ref, gmap_ref, wup_ref,
    force_ref, fgrad_ref,
    landed, part, heard, send_sem, recv_sem,
):
    me = lax.axis_index("dom")
    quarter = lax.axis_index("edge")
    barrier = greet(dom_size)
    pl.semaphore_wait(barrier, NOFF + QUART - 1)
    copies = []
    for number in range(NOFF):
        copy = pltpu.make_async_remote_copy(
            src_ref=gblocks_ref.at[number],
            dst_ref=landed.at[number],
            send_sem=send_sem.at[number],
            recv_sem=recv_sem.at[number],
            device_id=(neighbours(dom_size, number, -1), quarter),
            device_id_type=MESH,
        )
        copy.start()
        copies.append(copy)

    low = iota((64, 128), 1) < 64
    low16 = iota((16, 128), 1) < 64
    total = jnp.zeros((GROWS, ATOMS), F32)
    for p in range(PAIRS):
        copies[2 * p].wait_recv()
        copies[2 * p + 1].wait_recv()
        even = landed[2 * p].astype(F32)
        odd = landed[2 * p + 1].astype(F32)
        top = jnp.where(low, even[0:64], pltpu.roll(odd[0:64], 64, 1))
        bottom = jnp.where(low, pltpu.roll(even[0:64], 64, 1), odd[0:64])
        pos = jnp.where(low16, even[64:80], pltpu.roll(odd[64:80], 64, 1))
        left = jnp.concatenate([top, bottom, pos], axis=0).astype(BF16)
        row = pair_rows(gmap_ref, p)
        onehot = jnp.where(iota((ATOMS, 128), 0) == row, 1.0, 0.0).astype(BF16)
        total = total + mm_nt(left, onehot)
    feat = total[0:128] + gown_ref[0:128, :]
    pos = total[128:136] + total[136:144] + gown_ref[128:136, :]
    for j in range(QUART):
        span = slice(128 * j, 128 * j + 128)
        part[j, 0:128, :] = feat[:, span]
        part[j, 128:136, :] = pos[:, span]

    sums = []
    for j in range(1, QUART):
        peer = lax.rem(quarter + j, QUART)
        copy = pltpu.make_async_remote_copy(
            src_ref=part.at[peer],
            dst_ref=heard.at[j - 1],
            send_sem=send_sem.at[NOFF + j - 1],
            recv_sem=recv_sem.at[NOFF + j - 1],
            device_id=(me, peer),
            device_id_type=MESH,
        )
        copy.start()
        sums.append(copy)
    got = part[quarter]
    for j, copy in enumerate(sums):
        copy.wait_recv()
        got = got + heard[j]
    force_ref[...] = -got[128:131]
    fgrad_ref[...] = lax.dot_general(
        got[0:128].T,
        wup_ref[...].astype(F32),
        (((1,), (1,)), ((), ())),
        precision=HIGH,
        preferred_element_type=F32,
    )
    for copy in copies + sums:
        copy.wait_send()


def on_device(
    dom_size, coordinates, features, species, ghost_map, edge_sender, edge_receiver, edge_count,
    w_up, radial_one, radial_two, radial_three, read_mix, species_out,
):
    sds = jax.ShapeDtypeStruct
    edges = QUART * EDGE_ROWS
    slots, blocks, own = pl.pallas_call(
        lambda *refs: exchange_kernel(dom_size, *refs),
        out_shape=(sds((RANKS, OWN), I32), sds((NOFF, BLK, 128), BF16), sds((CH, ATOMS), BF16)),
        in_specs=[VMEM_SPEC] * 6 + [pl.BlockSpec(memory_space=pltpu.SMEM)],
        out_specs=(VMEM_SPEC,) * 3,
        scratch_shapes=[
            pltpu.VMEM((NOFF, BLK, 128), BF16),
            pltpu.VMEM((QUART, EDGE_ROWS, 128), I32),
            pltpu.VMEM((edges, 128), F32),
            pltpu.VMEM((edges, 128), F32),
            pltpu.VMEM((edges, 128), F32),
            pltpu.VMEM((256, 384), BF16),
            pltpu.SemaphoreType.DMA((NOFF + QUART - 1,)),
            pltpu.SemaphoreType.DMA((NOFF + QUART - 1,)),
        ],
        compiler_params=pltpu.CompilerParams(
            collective_id=0, has_side_effects=True, vmem_limit_bytes=LIMIT
        ),
        name="exchange",
    )(
        features, w_up, coordinates, ghost_map,
        edge_sender.reshape(EDGE_ROWS, 128), edge_receiver.reshape(EDGE_ROWS, 128), edge_count,
    )

    edge_total = OWN * RANKS
    energy, gblocks, gown = pl.pallas_call(
        compute_kernel,
        out_shape=(sds((1, OWN), F32), sds((NOFF, BLK, 128), BF16), sds((136, ATOMS), F32)),
        in_specs=[VMEM_SPEC] * 10,
        out_specs=(VMEM_SPEC,) * 3,
        scratch_shapes=[
            pltpu.VMEM((GROUPS * GROWS, 256), BF16),
            pltpu.VMEM((256, edge_total), BF16),
            pltpu.VMEM((9 * CH, OWN), F32),
            pltpu.VMEM((3 * CH, edge_total), F32),
            pltpu.VMEM((CH, edge_total), F32),
            pltpu.VMEM((64, edge_total), F32),
            pltpu.VMEM((64, edge_total), F32),
            pltpu.VMEM((8, edge_total), F32),
            pltpu.VMEM((8, edge_total), F32),
            pltpu.VMEM((GROUPS * GROWS, 256), F32),
            pltpu.VMEM((128, 128), F32),
            pltpu.VMEM((64, 24), BF16),
            pltpu.VMEM((64, 192), BF16),
            pltpu.VMEM((384, 192), BF16),
            pltpu.VMEM((8, 192), BF16),
            pltpu.VMEM((64, 192), BF16),
            pltpu.VMEM((128, 384), BF16),
            pltpu.VMEM((24, NE), F32),
        ],
        compiler_params=pltpu.CompilerParams(vmem_limit_bytes=LIMIT),
        name="compute",
    )(
        slots, blocks, own, coordinates, species.reshape(QUART, OWN),
        radial_one, radial_two, radial_three, read_mix, species_out,
    )

    forces, feature_grad = pl.pallas_call(
        lambda *refs: return_kernel(dom_size, *refs),
        out_shape=(sds((3, OWN), F32), sds((OWN, CH), F32)),
        in_specs=[VMEM_SPEC] * 4,
        out_specs=(VMEM_SPEC,) * 2,
        scratch_shapes=[
            pltpu.VMEM((NOFF, BLK, 128), BF16),
            pltpu.VMEM((QUART, 136, 128), F32),
            pltpu.VMEM((QUART - 1, 136, 128), F32),
            pltpu.SemaphoreType.DMA((NOFF + QUART - 1,)),
            pltpu.SemaphoreType.DMA((NOFF + QUART - 1,)),
        ],
        compiler_params=pltpu.CompilerParams(
            collective_id=1, has_side_effects=True, vmem_limit_bytes=LIMIT
        ),
        name="giveback",
    )(gblocks, gown, ghost_map, w_up)
    return energy.reshape(OWN), forces, feature_grad


def solution(mesh):
    dom_size = mesh.shape["dom"]
    return jax.shard_map(
        lambda *args: on_device(dom_size, *args),
        mesh=mesh,
        in_specs=(
            P(None, "dom"),
            P("dom", None),
            P("dom"),
            P("dom", None),
            P(("dom", "edge")),
            P(("dom", "edge")),
            P("dom"),
            P(),
            P(),
            P(),
            P(),
            P(),
            P(),
        ),
        out_specs=(P(("dom", "edge")), P(None, ("dom", "edge")), P(("dom", "edge"), None)),
        check_vma=False,
    )
```

```python
import jax
import jax.numpy as jnp
from jax import lax
from jax.experimental import pallas as pl
from jax.experimental.pallas import tpu as pltpu
from jax.sharding import PartitionSpec as P

F32, BF16, I32 = jnp.float32, jnp.bfloat16, jnp.int32
HIGH = lax.Precision.HIGHEST
MESH = pl.DeviceIdType.MESH
VMEM_SPEC = pl.BlockSpec(memory_space=pltpu.VMEM)

CH = 128
ATOMS = 512
OWN = 128
RANKS = 64
SLOT = 64
NOFF = 26
PAIRS = NOFF // 2
QUART = 4
EDGE_ROWS = 64
GROUPS = 9
GROWS = 144
PER = 16
NE = PER * OWN
STEPS = OWN * RANKS // NE
SORT_ROWS = 64
BLK = 80
SENTINEL = 4095
LIMIT = 56 * 1024 * 1024

OFFSETS = [
    (a, b, c)
    for a in (-1, 0, 1)
    for b in (-1, 0, 1)
    for c in (-1, 0, 1)
    if (a, b, c) != (0, 0, 0)
]


def shifts(count):
    side = 1
    while side * side * side < count:
        side += 1
    return [o[0] * side * side + o[1] * side + o[2] for o in OFFSETS]


def mm(a, b):
    return lax.dot_general(a, b, (((1,), (0,)), ((), ())), preferred_element_type=F32)


def mm_nt(a, b):
    return lax.dot_general(a, b, (((1,), (1,)), ((), ())), preferred_element_type=F32)


def mm_high(a, b):
    return lax.dot_general(
        a, b, (((1,), (0,)), ((), ())), precision=HIGH, preferred_element_type=F32
    )


def split(x):
    hi = x.astype(BF16)
    return hi, (x - hi.astype(F32)).astype(BF16)


def weight_stack(w):
    hi, lo = split(w)
    return jnp.concatenate([hi, hi, lo], axis=1)


def value_stack(x):
    hi, lo = split(x)
    return jnp.concatenate([hi, lo, hi], axis=0)


def iota(shape, dim):
    return lax.broadcasted_iota(I32, shape, dim)


def fold(x):
    parts = [x[:, 128 * j : 128 * (j + 1)] for j in range(x.shape[1] // 128)]
    while len(parts) > 1:
        parts = [parts[j] + parts[j + 1] for j in range(0, len(parts), 2)]
    return parts[0]


def map_rows(gmap_ref, core, i):
    other = min(i + 1, PAIRS - 1)
    return jnp.concatenate(
        [gmap_ref[pl.ds(2 * i + core, 1), :], gmap_ref[pl.ds(2 * other + core, 1), :]], axis=1
    )


def offset_device(dom_size, i, core, sign):
    me, quarter = lax.axis_index("dom"), lax.axis_index("edge")
    even, odd = [(shifts(dom_size)[2 * i + j] * sign) % dom_size for j in (0, 1)]
    swap_even, swap_odd = [int(OFFSETS[2 * i + j][2] != 0) for j in (0, 1)]
    there = lax.rem(me + even + core * (odd - even), dom_size)
    swap = swap_even + core * (swap_odd - swap_even)
    return there, lax.rem(quarter + 2 * swap, QUART)


def greet(dom_size):
    barrier = pltpu.get_barrier_semaphore()
    quarter = lax.axis_index("edge")
    me = lax.axis_index("dom")
    core = lax.rem(quarter, 2)
    for i in range(PAIRS):
        for sign in (1, -1):
            there = offset_device(dom_size, i, core, sign)
            pl.semaphore_signal(barrier, inc=1, device_id=there, device_id_type=MESH)
    for j in range(1, QUART):
        peer = lax.rem(quarter + j, QUART)
        pl.semaphore_signal(barrier, inc=1, device_id=(me, peer), device_id_type=MESH)
    return barrier


def exchange_kernel(
    dom_size,
    feat_ref, wup_ref, coord_ref, gmap_ref, snd_ref, rcv_ref, cnt_ref,
    slots_ref, blocks_ref, own_ref,
    sendblk, epack, li_s, g_s, hi_s, tri_s, send_sem, recv_sem,
):
    me = lax.axis_index("dom")
    quarter = lax.axis_index("edge")
    core = lax.rem(quarter, 2)
    mate = quarter + 1 - 2 * core
    barrier = greet(dom_size)

    first = quarter * (EDGE_ROWS * 128)
    index = first + iota((EDGE_ROWS, 128), 0) * 128 + iota((EDGE_ROWS, 128), 1)
    sender = jnp.where(index < cnt_ref[0], snd_ref[...], SENTINEL)
    epack[quarter] = sender + rcv_ref[...] * 65536

    hprime = mm(feat_ref[...], wup_ref[...]).astype(BF16)
    h_t = hprime.astype(F32).T.astype(BF16)
    own_ref[...] = h_t
    coords = jnp.concatenate(
        [coord_ref[...].astype(F32), jnp.zeros((13, ATOMS), F32)], axis=0
    ).astype(BF16)
    ext = jnp.concatenate([h_t, coords], axis=0)

    low = iota((64, 128), 1) < 64
    low16 = iota((16, 128), 1) < 64
    for i in range(0, PAIRS, 2):
        onehot = jnp.where(iota((ATOMS, 128), 0) == map_rows(gmap_ref, core, i), 1.0, 0.0)
        picked = mm(ext, onehot.astype(BF16))
        top, bottom, pos = picked[0:64], picked[64:128], picked[128:144]
        sendblk[i, 0:64, :] = jnp.where(low, top, pltpu.roll(bottom, 64, 1)).astype(BF16)
        sendblk[i, 64:80, :] = pos.astype(BF16)
        if i + 1 < PAIRS:
            sendblk[i + 1, 0:64, :] = jnp.where(low, pltpu.roll(top, 64, 1), bottom).astype(BF16)
            sendblk[i + 1, 64:80, :] = pltpu.roll(pos, 64, 1).astype(BF16)

    pl.semaphore_wait(barrier, NOFF + QUART - 1)

    copies = []
    for j in range(1, QUART):
        peer = lax.rem(quarter + j, QUART)
        copy = pltpu.make_async_remote_copy(
            src_ref=epack.at[quarter],
            dst_ref=epack.at[quarter],
            send_sem=send_sem.at[PAIRS + j - 1],
            recv_sem=recv_sem.at[PAIRS + j - 1],
            device_id=(me, peer),
            device_id_type=MESH,
        )
        copy.start()
        copies.append(copy)

    ghosts = []
    for j in range(PAIRS):
        copy = pltpu.make_async_remote_copy(
            src_ref=sendblk.at[j],
            dst_ref=blocks_ref.at[core, j],
            send_sem=send_sem.at[j],
            recv_sem=recv_sem.at[j],
            device_id=offset_device(dom_size, j, core, 1),
            device_id_type=MESH,
        )
        copy.start()
        ghosts.append(copy)

    for copy in copies:
        copy.wait_recv()

    packed = epack[...].reshape(QUART * EDGE_ROWS, 128)
    local = (packed >> 16) - quarter * OWN
    inside = (local >= 0) & (local < OWN)
    li_s[...] = jnp.where(inside, local, 255).astype(F32)
    value = packed & 65535
    g_s[...] = (value >> 8).astype(F32)
    hi_s[...] = (value & 255).astype(F32)
    tri_s[:, 0:256] = jnp.where(iota((256, 256), 0) < iota((256, 256), 1), 1.0, 0.0).astype(BF16)
    tri_s[:, 256:384] = jnp.ones((256, 128), BF16)

    atom = iota((OWN, 256), 0).astype(F32)
    rank_of = iota((RANKS, 256), 0).astype(F32)

    def sort_step(step, carry):
        base, total = carry
        rows = pl.ds(pl.multiple_of(step * SORT_ROWS, SORT_ROWS), SORT_ROWS)
        li8, g8, hi8 = li_s[rows, :], g_s[rows, :], hi_s[rows, :]

        def lane_row(x, b):
            return jnp.concatenate([x[2 * b : 2 * b + 1], x[2 * b + 1 : 2 * b + 2]], axis=1)

        hots = [jnp.where(atom == lane_row(li8, b), 1.0, 0.0) for b in range(SORT_ROWS // 2)]
        hots16 = [hot.astype(BF16) for hot in hots]
        counts = mm(jnp.concatenate(hots16, axis=0), tri_s[...])
        lefts = []
        for b in range(SORT_ROWS // 2):
            block = counts[OWN * b : OWN * (b + 1)]
            before = block[:, 0:256] + jnp.concatenate([base, base], axis=1)
            base = base + block[:, 256:384]
            rank = jnp.sum(before * hots[b], axis=0, keepdims=True)
            here = rank_of == rank
            lefts.append(
                jnp.concatenate(
                    [
                        jnp.where(here, lane_row(g8, b), 0.0).astype(BF16),
                        jnp.where(here, lane_row(hi8, b), 0.0).astype(BF16),
                    ],
                    axis=0,
                )
            )
        total = total + mm_nt(jnp.concatenate(lefts, axis=1), jnp.concatenate(hots16, axis=1))
        return base, total

    zero = jnp.zeros((OWN, 128), F32)
    steps = QUART * EDGE_ROWS // SORT_ROWS
    state = lax.fori_loop(0, steps // 2, sort_step, (zero, zero))
    for copy in ghosts:
        copy.wait_recv()
    share = pltpu.make_async_remote_copy(
        src_ref=blocks_ref.at[core],
        dst_ref=blocks_ref.at[core],
        send_sem=send_sem.at[PAIRS + QUART - 1],
        recv_sem=recv_sem.at[PAIRS + QUART - 1],
        device_id=(me, mate),
        device_id_type=MESH,
    )
    share.start()
    _, total = lax.fori_loop(steps // 2, steps, sort_step, state)
    slots_ref[...] = (total[0:64] * 256.0 + total[64:128]).astype(I32)
    share.wait_recv()
    for copy in copies + ghosts + [share]:
        copy.wait_send()


def compute_kernel(
    slots_ref, blocks_ref, own_ref, coord_ref, species_ref,
    w1_ref, w2_ref, w3_ref, mix_ref, sp_ref,
    energy_ref, gblocks_ref, gown_ref,
    tab, hot_s, acc, rad_s, h_s, d1_s, d2_s, bas_s, row_s, scat, sp_s,
    w1f, w2f, w3f, w1b, w2b, w3b, myc,
):
    quarter = lax.axis_index("edge")
    lane = iota((64, 128), 1)
    low = lane < 64
    low8 = iota((8, 128), 1) < 64
    low16 = iota((16, 128), 1) < 64
    sub8 = iota((8, 128), 0)

    coords = coord_ref[...].astype(F32)
    coords16 = jnp.concatenate([coords, jnp.zeros((13, ATOMS), F32)], axis=0).astype(BF16)
    for g in range(2):
        tab[GROWS * g : GROWS * g + 128, :] = own_ref[:, 256 * g : 256 * g + 256]
        tab[GROWS * g + 128 : GROWS * (g + 1), :] = coords16[:, 256 * g : 256 * g + 256]
    tab[GROWS * 8 : GROWS * 9, :] = jnp.zeros((GROWS, 256), BF16)
    for p in range(PAIRS):
        g, at = 2 + p // 2, 128 * (p % 2)
        even = blocks_ref[0, p].astype(F32)
        odd = blocks_ref[1, p].astype(F32)
        top = jnp.where(low, even[0:64], pltpu.roll(odd[0:64], 64, 1))
        bottom = jnp.where(low, pltpu.roll(even[0:64], 64, 1), odd[0:64])
        pos = jnp.where(low16, even[64:80], pltpu.roll(odd[64:80], 64, 1))
        oe, oo = OFFSETS[2 * p], OFFSETS[2 * p + 1]
        off = jnp.zeros((16, 128), F32)
        sub16 = iota((16, 128), 0)
        for c in range(3):
            if oe[c] != 0 or oo[c] != 0:
                off = jnp.where(sub16 == 3 + c, jnp.where(low16, float(oe[c]), float(oo[c])), off)
        pos = pos + off
        tab[GROWS * g : GROWS * g + 64, at : at + 128] = top.astype(BF16)
        tab[GROWS * g + 64 : GROWS * g + 128, at : at + 128] = bottom.astype(BF16)
        tab[GROWS * g + 128 : GROWS * (g + 1), at : at + 128] = pos.astype(BF16)

    w1f[...] = weight_stack(w1_ref[...].T)
    w2f[...] = weight_stack(w2_ref[...].T)
    w3f[...] = weight_stack(w3_ref[...].T)
    w1b[...] = weight_stack(w1_ref[...])
    w2b[...] = weight_stack(w2_ref[...])
    hi, lo = split(w3_ref[...])
    w3b[...] = jnp.concatenate([hi, lo], axis=0)

    acc[...] = jnp.zeros(acc.shape, F32)
    scat[...] = jnp.zeros(scat.shape, F32)
    mine = pl.ds(pl.multiple_of(quarter * OWN, OWN), OWN)
    my_coords = coord_ref[:, mine].astype(F32)
    for c in range(3):
        mc = jnp.broadcast_to(my_coords[c : c + 1], (8, 128))
        myc[8 * c : 8 * c + 8, :] = jnp.concatenate([mc] * PER, axis=1)

    beta = jnp.zeros((8, NE), F32)
    for n in range(8):
        beta = jnp.where(iota((8, NE), 0) == n, 0.4 * 15.0 ** (n / 7.0), beta)

    def slot_row(step):
        s = jnp.concatenate(
            [slots_ref[pl.ds(PER * step + j, 1), :] for j in range(PER)], axis=1
        )
        return jnp.broadcast_to(s, (8, NE))

    def harmonic(x, y, z, dsq):
        third = dsq * (1.0 / 3.0)
        return [None, x, y, z, x * y, y * z, x * z, x * x - third, y * y - third]

    degree = [0, 1, 1, 1, 2, 2, 2, 2, 2]

    def fwd(step, carry):
        lanes = pl.ds(pl.multiple_of(step * NE, NE), NE)
        s = slot_row(step)
        group = s >> 8
        hi = s & 255
        valid = jnp.where(group < GROUPS, 1.0, 0.0)
        sub = iota((8, NE), 0)
        onehot = jnp.concatenate(
            [jnp.where(sub + 8 * t == hi, 1.0, 0.0) for t in range(32)], axis=0
        ).astype(BF16)
        hot_s[:, lanes] = onehot
        got = mm(tab[...], onehot)
        masks = [group == k for k in range(GROUPS)]
        rows = []
        for t in range(17):
            v = jnp.zeros((8, NE), F32)
            for k in range(GROUPS):
                at = GROWS * k + 8 * t
                v = jnp.where(masks[k], got[at : at + 8], v)
            rows.append(v)
        pos = rows[16]
        rel = []
        for c in range(3):
            sent = pos[c : c + 1] - pos[3 + c : 4 + c]
            rel.append(jnp.broadcast_to(sent, (8, NE)) - myc[8 * c : 8 * c + 8, :])
        x, y, z = rel
        dsq = x * x + y * y + z * z
        e0 = jnp.maximum(0.0, 1.0 - dsq * 0.25) * valid
        env = e0 * e0
        basis = jnp.exp(-dsq * beta)
        packed = jnp.zeros((8, NE), F32)
        for j, v in enumerate((x, y, z, dsq, env, e0)):
            packed = jnp.where(sub == j, v, packed)
        row_s[:, lanes] = packed
        bas_s[:, lanes] = basis

        def act(pre):
            sig = 0.5 + 0.5 * jnp.tanh(0.5 * pre)
            out = pre * sig
            return out, sig + out * (1.0 - sig)

        h1, d1 = act(mm(w1f[...], value_stack(basis)))
        d1_s[:, lanes] = d1
        h2, d2 = act(mm(w2f[...], value_stack(h1)))
        d2_s[:, lanes] = d2
        rad = mm(w3f[...], value_stack(h2))
        rad_s[:, lanes] = rad
        ys = harmonic(x, y, z, dsq)
        for t in range(16):
            h = rows[t]
            h_s[8 * t : 8 * t + 8, lanes] = h
            he = h * env
            ds = [he * rad[128 * l + 8 * t : 128 * l + 8 * t + 8] for l in range(3)]
            for m in range(9):
                msg = ds[degree[m]] if m == 0 else ds[degree[m]] * ys[m]
                at = 128 * m + 8 * t
                acc[at : at + 8, :] += fold(msg)
        return carry

    lax.fori_loop(0, STEPS, fwd, 0)

    def node(m):
        return acc[128 * m : 128 * m + 128, :] * 0.125

    a0, vx, vy, vz, xy, yz, xz, xx, yy = [node(m) for m in range(9)]
    zz = -xx - yy
    n1 = vx * vx + vy * vy + vz * vz
    n2 = xx * xx + yy * yy + zz * zz + 2.0 * (xy * xy + yz * yz + xz * xz)
    cx = xx * vx + xy * vy + xz * vz
    cy = xy * vx + yy * vy + yz * vz
    cz = xz * vx + yz * vy + zz * vz
    cub = cx * vx + cy * vy + cz * vz
    inv = jnp.concatenate([a0, n1, n2, a0 * n1, cub], axis=0)
    pre = mm_high(mix_ref[...].T, inv)
    sig = 0.5 + 0.5 * jnp.tanh(0.5 * pre)
    hid = pre * sig
    sp_s[...] = jnp.zeros((128, 128), F32)
    sp_s[0:89, :] = sp_ref[...]
    kinds = species_ref[pl.ds(quarter, 1), :]
    kind_hot = jnp.where(iota((128, 128), 0) == kinds, 1.0, 0.0)
    per_kind = mm_high(sp_s[...].T, kind_hot)
    energy_ref[...] = jnp.sum(hid * per_kind, axis=0, keepdims=True)
    dpre = per_kind * (sig + hid * (1.0 - sig))
    dinv = mm_high(mix_ref[...], dpre) * 0.125
    g0, g1, g2, g3, g4 = [dinv[128 * j : 128 * j + 128] for j in range(5)]
    w = 2.0 * (g1 + g3 * a0)
    c2 = 2.0 * g4
    acc[0:128, :] = g0 + g3 * n1
    acc[128:256, :] = w * vx + c2 * cx
    acc[256:384, :] = w * vy + c2 * cy
    acc[384:512, :] = w * vz + c2 * cz
    acc[512:640, :] = 4.0 * xy * g2 + c2 * vx * vy
    acc[640:768, :] = 4.0 * yz * g2 + c2 * vy * vz
    acc[768:896, :] = 4.0 * xz * g2 + c2 * vx * vz
    acc[896:1024, :] = 2.0 * g2 * (xx - zz) + g4 * (vx * vx - vz * vz)
    acc[1024:1152, :] = 2.0 * g2 * (yy - zz) + g4 * (vy * vy - vz * vz)

    def bwd(step, down):
        lanes = pl.ds(pl.multiple_of(step * NE, NE), NE)
        group = slot_row(step) >> 8
        rows = row_s[:, lanes]
        x, y, z, dsq, env, e0 = [jnp.broadcast_to(rows[j : j + 1], (8, NE)) for j in range(6)]
        ys = harmonic(x, y, z, dsq)
        denv = jnp.zeros((8, NE), F32)
        dys = [jnp.zeros((8, NE), F32) for _ in range(9)]
        dhs, drs = [], [[], [], []]
        for t in range(16):
            da = []
            for m in range(9):
                v = acc[128 * m + 8 * t : 128 * m + 8 * t + 8, :]
                da.append(jnp.concatenate([v] * PER, axis=1))
            t0 = da[0]
            t1 = x * da[1] + y * da[2] + z * da[3]
            t2 = ys[4] * da[4]
            for m in range(5, 9):
                t2 = t2 + ys[m] * da[m]
            ts = [t0, t1, t2]
            rs = [rad_s[128 * l + 8 * t : 128 * l + 8 * t + 8, lanes] for l in range(3)]
            u = rs[0] * t0 + rs[1] * t1 + rs[2] * t2
            h = h_s[8 * t : 8 * t + 8, lanes]
            he = h * env
            denv = denv + h * u
            dhs.append(env * u)
            for l in range(3):
                drs[l].append(he * ts[l])
            d1, d2 = he * rs[1], he * rs[2]
            for m in range(1, 9):
                dys[m] = dys[m] + (d1 if m < 4 else d2) * da[m]

        def total(v):
            return jnp.broadcast_to(jnp.sum(v, axis=0, keepdims=True), (8, NE))

        drad = jnp.concatenate(drs[0] + drs[1] + drs[2], axis=0).astype(BF16)
        both = mm(w3b[...], drad)
        dp2 = (both[0:64] + both[64:128]) * d2_s[:, lanes]
        dp1 = mm(w2b[...], value_stack(dp2)) * d1_s[:, lanes]
        dbas = mm(w1b[...], value_stack(dp1))
        denv = total(denv)
        dys = [None] + [total(v) for v in dys[1:]]
        ddsq = (
            -total(dbas * bas_s[:, lanes] * beta)
            - 0.5 * e0 * denv
            - (dys[7] + dys[8]) * (1.0 / 3.0)
        )
        two = 2.0 * ddsq
        dx = dys[1] + y * dys[4] + z * dys[6] + 2.0 * x * dys[7] + x * two
        dy = dys[2] + x * dys[4] + z * dys[5] + 2.0 * y * dys[8] + y * two
        dz = dys[3] + y * dys[5] + x * dys[6] + z * two
        sub = iota((8, NE), 0)
        drel = jnp.where(sub == 0, dx, jnp.where(sub == 1, dy, jnp.where(sub == 2, dz, 0.0)))
        drel_hi = drel.astype(BF16).astype(F32)
        flow = jnp.concatenate(dhs + [drel_hi, drel - drel_hi], axis=0).astype(BF16)
        group16 = jnp.concatenate([group, group], axis=0)
        lefts = []
        for k in range(GROUPS):
            mask = jnp.where(group16 == k, 1.0, 0.0).astype(BF16)
            lefts.extend(flow[16 * t : 16 * t + 16] * mask for t in range(9))
        scat[...] += mm_nt(jnp.concatenate(lefts, axis=0), hot_s[:, lanes])
        return down + fold(drel)

    down = lax.fori_loop(0, STEPS, bwd, jnp.zeros((8, 128), F32))

    for g in range(2):
        span = slice(256 * g, 256 * g + 256)
        gown_ref[0:128, span] = scat[GROWS * g : GROWS * g + 128, :]
        gown_ref[128:136, span] = (
            scat[GROWS * g + 128 : GROWS * g + 136, :] + scat[GROWS * g + 136 : GROWS * g + 144, :]
        )
    gown_ref[128:136, mine] = gown_ref[128:136, mine] - down
    for p in range(PAIRS):
        g, at = 2 + p // 2, 128 * (p % 2)
        top = scat[GROWS * g : GROWS * g + 64, at : at + 128]
        bottom = scat[GROWS * g + 64 : GROWS * g + 128, at : at + 128]
        pos = (
            scat[GROWS * g + 128 : GROWS * g + 136, at : at + 128]
            + scat[GROWS * g + 136 : GROWS * g + 144, at : at + 128]
        )
        pos_hi = pos.astype(BF16).astype(F32)
        pos = jnp.concatenate([pos_hi, pos - pos_hi], axis=0)
        even = jnp.where(low, top, pltpu.roll(bottom, 64, 1))
        odd = jnp.where(low, pltpu.roll(top, 64, 1), bottom)
        gblocks_ref[0, p, 0:64, :] = even.astype(BF16)
        gblocks_ref[1, p, 0:64, :] = odd.astype(BF16)
        gblocks_ref[0, p, 64:80, :] = jnp.where(low16, pos, 0.0).astype(BF16)
        gblocks_ref[1, p, 64:80, :] = jnp.where(low16, pltpu.roll(pos, 64, 1), 0.0).astype(BF16)


def landed_block(copies, landed, i):
    copies[i].wait_recv()
    return landed[i].astype(F32)


def return_kernel(
    dom_size,
    gblocks_ref, gown_ref, gmap_ref, wup_ref,
    force_ref, fgrad_ref,
    matebuf, sendblk, landed, part, heard, send_sem, recv_sem,
):
    me = lax.axis_index("dom")
    quarter = lax.axis_index("edge")
    core = lax.rem(quarter, 2)
    mate = quarter + 1 - 2 * core
    barrier = greet(dom_size)
    pl.semaphore_wait(barrier, NOFF + QUART - 1)
    share = pltpu.make_async_remote_copy(
        src_ref=gblocks_ref.at[1 - core],
        dst_ref=matebuf,
        send_sem=send_sem.at[PAIRS + QUART - 1],
        recv_sem=recv_sem.at[PAIRS + QUART - 1],
        device_id=(me, mate),
        device_id_type=MESH,
    )
    share.start()
    share.wait_recv()
    copies = []
    for i in range(PAIRS):
        sendblk[i] = (gblocks_ref[core, i].astype(F32) + matebuf[i].astype(F32)).astype(BF16)
        copy = pltpu.make_async_remote_copy(
            src_ref=sendblk.at[i],
            dst_ref=landed.at[i],
            send_sem=send_sem.at[i],
            recv_sem=recv_sem.at[i],
            device_id=offset_device(dom_size, i, core, -1),
            device_id_type=MESH,
        )
        copy.start()
        copies.append(copy)

    low = iota((64, 128), 1) < 64
    low16 = iota((16, 128), 1) < 64
    total = jnp.zeros((GROWS, ATOMS), F32)
    for i in range(0, PAIRS, 2):
        even = landed_block(copies, landed, i)
        odd = landed_block(copies, landed, i + 1) if i + 1 < PAIRS else jnp.zeros((BLK, 128), F32)
        top = jnp.where(low, even[0:64], pltpu.roll(odd[0:64], 64, 1))
        bottom = jnp.where(low, pltpu.roll(even[0:64], 64, 1), odd[0:64])
        pos = jnp.where(low16, even[64:80], pltpu.roll(odd[64:80], 64, 1))
        left = jnp.concatenate([top, bottom, pos], axis=0).astype(BF16)
        onehot = jnp.where(iota((ATOMS, 128), 0) == map_rows(gmap_ref, core, i), 1.0, 0.0)
        total = total + mm_nt(left, onehot.astype(BF16))
    feat = total[0:128] + gown_ref[0:128, :]
    pos = total[128:136] + total[136:144] + gown_ref[128:136, :]
    for j in range(QUART):
        span = slice(128 * j, 128 * j + 128)
        part[j, 0:128, :] = feat[:, span]
        part[j, 128:136, :] = pos[:, span]

    sums = []
    for j in range(1, QUART):
        peer = lax.rem(quarter + j, QUART)
        copy = pltpu.make_async_remote_copy(
            src_ref=part.at[peer],
            dst_ref=heard.at[j - 1],
            send_sem=send_sem.at[PAIRS + j - 1],
            recv_sem=recv_sem.at[PAIRS + j - 1],
            device_id=(me, peer),
            device_id_type=MESH,
        )
        copy.start()
        sums.append(copy)
    got = part[quarter]
    for j, copy in enumerate(sums):
        copy.wait_recv()
        got = got + heard[j]
    force_ref[...] = -got[128:131]
    fgrad_ref[...] = lax.dot_general(
        got[0:128].T,
        wup_ref[...].astype(F32),
        (((1,), (1,)), ((), ())),
        precision=HIGH,
        preferred_element_type=F32,
    )
    for copy in copies + sums + [share]:
        copy.wait_send()


def compute_call(*operands):
    sds = jax.ShapeDtypeStruct
    edge_total = OWN * RANKS
    return pl.pallas_call(
        compute_kernel,
        out_shape=(sds((1, OWN), F32), sds((2, PAIRS, BLK, 128), BF16), sds((136, ATOMS), F32)),
        in_specs=[VMEM_SPEC] * 10,
        out_specs=(VMEM_SPEC,) * 3,
        scratch_shapes=[
            pltpu.VMEM((GROUPS * GROWS, 256), BF16),
            pltpu.VMEM((256, edge_total), BF16),
            pltpu.VMEM((9 * CH, OWN), F32),
            pltpu.VMEM((3 * CH, edge_total), F32),
            pltpu.VMEM((CH, edge_total), F32),
            pltpu.VMEM((64, edge_total), F32),
            pltpu.VMEM((64, edge_total), F32),
            pltpu.VMEM((8, edge_total), F32),
            pltpu.VMEM((8, edge_total), F32),
            pltpu.VMEM((GROUPS * GROWS, 256), F32),
            pltpu.VMEM((128, 128), F32),
            pltpu.VMEM((64, 24), BF16),
            pltpu.VMEM((64, 192), BF16),
            pltpu.VMEM((384, 192), BF16),
            pltpu.VMEM((8, 192), BF16),
            pltpu.VMEM((64, 192), BF16),
            pltpu.VMEM((128, 384), BF16),
            pltpu.VMEM((24, NE), F32),
        ],
        compiler_params=pltpu.CompilerParams(vmem_limit_bytes=LIMIT),
        name="compute",
    )(*operands)


def exchange_call(dom_size, *operands):
    sds = jax.ShapeDtypeStruct
    edges = QUART * EDGE_ROWS
    return pl.pallas_call(
        lambda *refs: exchange_kernel(dom_size, *refs),
        out_shape=(sds((RANKS, OWN), I32), sds((2, PAIRS, BLK, 128), BF16), sds((CH, ATOMS), BF16)),
        in_specs=[VMEM_SPEC] * 6 + [pl.BlockSpec(memory_space=pltpu.SMEM)],
        out_specs=(VMEM_SPEC,) * 3,
        scratch_shapes=[
            pltpu.VMEM((PAIRS, BLK, 128), BF16),
            pltpu.VMEM((QUART, EDGE_ROWS, 128), I32),
            pltpu.VMEM((edges, 128), F32),
            pltpu.VMEM((edges, 128), F32),
            pltpu.VMEM((edges, 128), F32),
            pltpu.VMEM((256, 384), BF16),
            pltpu.SemaphoreType.DMA((PAIRS + QUART,)),
            pltpu.SemaphoreType.DMA((PAIRS + QUART,)),
        ],
        compiler_params=pltpu.CompilerParams(
            collective_id=0, has_side_effects=True, vmem_limit_bytes=LIMIT
        ),
        name="exchange",
    )(*operands)


def giveback_call(dom_size, *operands):
    sds = jax.ShapeDtypeStruct
    return pl.pallas_call(
        lambda *refs: return_kernel(dom_size, *refs),
        out_shape=(sds((3, OWN), F32), sds((OWN, CH), F32)),
        in_specs=[VMEM_SPEC] * 4,
        out_specs=(VMEM_SPEC,) * 2,
        scratch_shapes=[
            pltpu.VMEM((PAIRS, BLK, 128), BF16),
            pltpu.VMEM((PAIRS, BLK, 128), BF16),
            pltpu.VMEM((PAIRS, BLK, 128), BF16),
            pltpu.VMEM((QUART, 136, 128), F32),
            pltpu.VMEM((QUART - 1, 136, 128), F32),
            pltpu.SemaphoreType.DMA((PAIRS + QUART,)),
            pltpu.SemaphoreType.DMA((PAIRS + QUART,)),
        ],
        compiler_params=pltpu.CompilerParams(
            collective_id=1, has_side_effects=True, vmem_limit_bytes=LIMIT
        ),
        name="giveback",
    )(*operands)


def on_device(
    dom_size, coordinates, features, species, ghost_map, edge_sender, edge_receiver, edge_count,
    w_up, radial_one, radial_two, radial_three, read_mix, species_out,
):
    slots, blocks, own = exchange_call(
        dom_size, features, w_up, coordinates, ghost_map,
        edge_sender.reshape(EDGE_ROWS, 128), edge_receiver.reshape(EDGE_ROWS, 128), edge_count,
    )
    energy, gblocks, gown = compute_call(
        slots, blocks, own, coordinates, species.reshape(QUART, OWN),
        radial_one, radial_two, radial_three, read_mix, species_out,
    )
    forces, feature_grad = giveback_call(dom_size, gblocks, gown, ghost_map, w_up)
    return energy.reshape(OWN), forces, feature_grad


def solution(mesh):
    dom_size = mesh.shape["dom"]
    return jax.shard_map(
        lambda *args: on_device(dom_size, *args),
        mesh=mesh,
        in_specs=(
            P(None, "dom"),
            P("dom", None),
            P("dom"),
            P("dom", None),
            P(("dom", "edge")),
            P(("dom", "edge")),
            P("dom"),
            P(),
            P(),
            P(),
            P(),
            P(),
            P(),
        ),
        out_specs=(P(("dom", "edge")), P(None, ("dom", "edge")), P(("dom", "edge"), None)),
        check_vma=False,
    )
```

```python
import jax
import jax.numpy as jnp
from jax import lax
from jax.experimental import pallas as pl
from jax.experimental.pallas import tpu as pltpu
from jax.sharding import PartitionSpec as P

F32, BF16, I32 = jnp.float32, jnp.bfloat16, jnp.int32
HIGH = lax.Precision.HIGHEST
MESH = pl.DeviceIdType.MESH
VMEM_SPEC = pl.BlockSpec(memory_space=pltpu.VMEM)

CH = 128
ATOMS = 512
OWN = 128
RANKS = 64
SLOT = 64
NOFF = 26
PAIRS = NOFF // 2
QUART = 4
EDGE_ROWS = 64
GROUPS = 9
GROWS = 144
TROWS = 1232
PER = 16
NE = PER * OWN
STEPS = OWN * RANKS // NE
SORT_ROWS = 64
BLK = 80
SENTINEL = 4095
LIMIT = 56 * 1024 * 1024

OFFSETS = [
    (a, b, c)
    for a in (-1, 0, 1)
    for b in (-1, 0, 1)
    for c in (-1, 0, 1)
    if (a, b, c) != (0, 0, 0)
]


def shifts(count):
    side = 1
    while side * side * side < count:
        side += 1
    return [o[0] * side * side + o[1] * side + o[2] for o in OFFSETS]


def mm(a, b):
    return lax.dot_general(a, b, (((1,), (0,)), ((), ())), preferred_element_type=F32)


def mm_nt(a, b):
    return lax.dot_general(a, b, (((1,), (1,)), ((), ())), preferred_element_type=F32)


def mm_high(a, b):
    return lax.dot_general(
        a, b, (((1,), (0,)), ((), ())), precision=HIGH, preferred_element_type=F32
    )


def split(x):
    hi = x.astype(BF16)
    return hi, (x - hi.astype(F32)).astype(BF16)


def weight_stack(w):
    hi, lo = split(w)
    return jnp.concatenate([hi, hi, lo], axis=1)


def value_stack(x):
    hi, lo = split(x)
    return jnp.concatenate([hi, lo, hi], axis=0)


def iota(shape, dim):
    return lax.broadcasted_iota(I32, shape, dim)


def fold(x):
    parts = [x[:, 128 * j : 128 * (j + 1)] for j in range(x.shape[1] // 128)]
    while len(parts) > 1:
        parts = [parts[j] + parts[j + 1] for j in range(0, len(parts), 2)]
    return parts[0]


def map_rows(gmap_ref, core, i):
    other = min(i + 1, PAIRS - 1)
    return jnp.concatenate(
        [gmap_ref[pl.ds(2 * i + core, 1), :], gmap_ref[pl.ds(2 * other + core, 1), :]], axis=1
    )


def offset_device(dom_size, i, core, sign):
    me, quarter = lax.axis_index("dom"), lax.axis_index("edge")
    even, odd = [(shifts(dom_size)[2 * i + j] * sign) % dom_size for j in (0, 1)]
    swap_even, swap_odd = [int(OFFSETS[2 * i + j][2] != 0) for j in (0, 1)]
    there = lax.rem(me + even + core * (odd - even), dom_size)
    swap = swap_even + core * (swap_odd - swap_even)
    return there, lax.rem(quarter + 2 * swap, QUART)


def greet(dom_size):
    barrier = pltpu.get_barrier_semaphore()
    quarter = lax.axis_index("edge")
    me = lax.axis_index("dom")
    core = lax.rem(quarter, 2)
    for i in range(PAIRS):
        for sign in (1, -1):
            there = offset_device(dom_size, i, core, sign)
            pl.semaphore_signal(barrier, inc=1, device_id=there, device_id_type=MESH)
    for j in range(1, QUART):
        peer = lax.rem(quarter + j, QUART)
        pl.semaphore_signal(barrier, inc=1, device_id=(me, peer), device_id_type=MESH)
    return barrier


def landed_block(copies, landed, i):
    copies[i].wait_recv()
    return landed[i].astype(F32)


def interaction_kernel(
    dom_size,
    feat_ref, wup_ref, coord_ref, gmap_ref, snd_ref, rcv_ref, cnt_ref, species_ref,
    w1_ref, w2_ref, w3_ref, mix_ref, sp_ref,
    energy_ref, grad_ref,
    slots_ref, blocks_ref, own_ref, gblocks_ref, gown_ref,
    sendblk, epack, li_s, g_s, hi_s, tri_s,
    tab, tab32, dh_s, hot_s, acc, rad_s, h_s, d1_s, d2_s, bas_s, row_s, scat, sp_s,
    w1f, w2f, w3f, w1b, w2b, w3b, myc,
    matebuf, backblk, landed, part, heard, send_sem, recv_sem, back_send_sem, back_recv_sem,
):
    me = lax.axis_index("dom")
    quarter = lax.axis_index("edge")
    core = lax.rem(quarter, 2)
    mate = quarter + 1 - 2 * core
    barrier = greet(dom_size)

    first = quarter * (EDGE_ROWS * 128)
    index = first + iota((EDGE_ROWS, 128), 0) * 128 + iota((EDGE_ROWS, 128), 1)
    sender = jnp.where(index < cnt_ref[0], snd_ref[...], SENTINEL)
    epack[quarter] = sender + rcv_ref[...] * 65536

    hprime = mm(feat_ref[...], wup_ref[...]).astype(BF16)
    h_t = hprime.astype(F32).T.astype(BF16)
    own_ref[...] = h_t
    coords = jnp.concatenate(
        [coord_ref[...].astype(F32), jnp.zeros((13, ATOMS), F32)], axis=0
    ).astype(BF16)
    ext = jnp.concatenate([h_t, coords], axis=0)

    low = iota((64, 128), 1) < 64
    low16 = iota((16, 128), 1) < 64
    low8 = iota((8, 128), 1) < 64
    sub8 = iota((8, 128), 0)
    for i in range(0, PAIRS, 2):
        onehot = jnp.where(iota((ATOMS, 128), 0) == map_rows(gmap_ref, core, i), 1.0, 0.0)
        picked = mm(ext, onehot.astype(BF16))
        top, bottom, pos = picked[0:64], picked[64:128], picked[128:144]
        sendblk[i, 0:64, :] = jnp.where(low, top, pltpu.roll(bottom, 64, 1)).astype(BF16)
        sendblk[i, 64:80, :] = pos.astype(BF16)
        if i + 1 < PAIRS:
            sendblk[i + 1, 0:64, :] = jnp.where(low, pltpu.roll(top, 64, 1), bottom).astype(BF16)
            sendblk[i + 1, 64:80, :] = pltpu.roll(pos, 64, 1).astype(BF16)

    pl.semaphore_wait(barrier, NOFF + QUART - 1)

    copies = []
    for j in range(1, QUART):
        peer = lax.rem(quarter + j, QUART)
        copy = pltpu.make_async_remote_copy(
            src_ref=epack.at[quarter],
            dst_ref=epack.at[quarter],
            send_sem=send_sem.at[PAIRS + j - 1],
            recv_sem=recv_sem.at[PAIRS + j - 1],
            device_id=(me, peer),
            device_id_type=MESH,
        )
        copy.start()
        copies.append(copy)

    ghosts = []
    for j in range(PAIRS):
        copy = pltpu.make_async_remote_copy(
            src_ref=sendblk.at[j],
            dst_ref=blocks_ref.at[core, j],
            send_sem=send_sem.at[j],
            recv_sem=recv_sem.at[j],
            device_id=offset_device(dom_size, j, core, 1),
            device_id_type=MESH,
        )
        copy.start()
        ghosts.append(copy)

    coords = coord_ref[...].astype(F32)
    coords8 = jnp.concatenate([coords, jnp.zeros((5, ATOMS), F32)], axis=0)
    def place(g, lanes, rows):
        for t in range(17):
            tab32[8 * (GROUPS * t + g) : 8 * (GROUPS * t + g) + 8, lanes] = rows[8 * t : 8 * t + 8]

    for g in range(2):
        span = slice(256 * g, 256 * g + 256)
        place(g, slice(0, 256), jnp.concatenate([own_ref[:, span].astype(F32), coords8[:, span]], axis=0))
    place(8, slice(0, 256), jnp.zeros((136, 256), F32))
    tab32[8 * GROUPS * 17 :, :] = jnp.zeros((TROWS - 8 * GROUPS * 17, 256), F32)
    w1f[...] = weight_stack(w1_ref[...].T)
    w2f[...] = weight_stack(w2_ref[...].T)
    w3f[...] = weight_stack(w3_ref[...].T)
    w1b[...] = weight_stack(w1_ref[...])
    w2b[...] = weight_stack(w2_ref[...])
    hi, lo = split(w3_ref[...])
    w3b[...] = jnp.concatenate([hi, lo], axis=0)

    acc[...] = jnp.zeros(acc.shape, F32)
    scat[...] = jnp.zeros(scat.shape, F32)
    mine = pl.ds(pl.multiple_of(quarter * OWN, OWN), OWN)
    my_coords = coord_ref[:, mine].astype(F32)
    for c in range(3):
        mc = jnp.broadcast_to(my_coords[c : c + 1], (8, 128))
        myc[8 * c : 8 * c + 8, :] = jnp.concatenate([mc] * PER, axis=1)

    beta = jnp.zeros((8, NE), F32)
    for n in range(8):
        beta = jnp.where(iota((8, NE), 0) == n, 0.4 * 15.0 ** (n / 7.0), beta)

    sp_s[...] = jnp.zeros((128, 128), F32)
    sp_s[0:89, :] = sp_ref[...]

    for copy in copies:
        copy.wait_recv()

    packed = epack[...].reshape(QUART * EDGE_ROWS, 128)
    local = (packed >> 16) - quarter * OWN
    inside = (local >= 0) & (local < OWN)
    li_s[...] = jnp.where(inside, local, 255).astype(F32)
    value = packed & 65535
    g_s[...] = (value >> 8).astype(F32)
    hi_s[...] = (value & 255).astype(F32)
    tri_s[:, 0:256] = jnp.where(iota((256, 256), 0) < iota((256, 256), 1), 1.0, 0.0).astype(BF16)
    tri_s[:, 256:384] = jnp.ones((256, 128), BF16)

    atom = iota((OWN, 256), 0).astype(F32)
    rank_of = iota((RANKS, 256), 0).astype(F32)

    def sort_step(step, carry):
        base, total = carry
        rows = pl.ds(pl.multiple_of(step * SORT_ROWS, SORT_ROWS), SORT_ROWS)
        li8, g8, hi8 = li_s[rows, :], g_s[rows, :], hi_s[rows, :]

        def lane_row(x, b):
            return jnp.concatenate([x[2 * b : 2 * b + 1], x[2 * b + 1 : 2 * b + 2]], axis=1)

        hots = [jnp.where(atom == lane_row(li8, b), 1.0, 0.0) for b in range(SORT_ROWS // 2)]
        hots16 = [hot.astype(BF16) for hot in hots]
        counts = mm(jnp.concatenate(hots16, axis=0), tri_s[...])
        lefts = []
        for b in range(SORT_ROWS // 2):
            block = counts[OWN * b : OWN * (b + 1)]
            before = block[:, 0:256] + jnp.concatenate([base, base], axis=1)
            base = base + block[:, 256:384]
            rank = jnp.sum(before * hots[b], axis=0, keepdims=True)
            here = rank_of == rank
            lefts.append(
                jnp.concatenate(
                    [
                        jnp.where(here, lane_row(g8, b), 0.0).astype(BF16),
                        jnp.where(here, lane_row(hi8, b), 0.0).astype(BF16),
                    ],
                    axis=0,
                )
            )
        total = total + mm_nt(jnp.concatenate(lefts, axis=1), jnp.concatenate(hots16, axis=1))
        return base, total

    zero = jnp.zeros((OWN, 128), F32)
    steps = QUART * EDGE_ROWS // SORT_ROWS
    state = lax.fori_loop(0, steps // 2, sort_step, (zero, zero))
    for copy in ghosts:
        copy.wait_recv()
    share = pltpu.make_async_remote_copy(
        src_ref=blocks_ref.at[core],
        dst_ref=blocks_ref.at[core],
        send_sem=send_sem.at[PAIRS + QUART - 1],
        recv_sem=recv_sem.at[PAIRS + QUART - 1],
        device_id=(me, mate),
        device_id_type=MESH,
    )
    share.start()
    _, total = lax.fori_loop(steps // 2, steps, sort_step, state)
    slots_ref[...] = (total[0:64] * 256.0 + total[64:128]).astype(I32)
    share.wait_recv()
    for copy in copies + ghosts + [share]:
        copy.wait_send()


    for p in range(PAIRS):
        g, at = 2 + p // 2, 128 * (p % 2)
        even = blocks_ref[0, p].astype(F32)
        odd = blocks_ref[1, p].astype(F32)
        top = jnp.where(low, even[0:64], pltpu.roll(odd[0:64], 64, 1))
        bottom = jnp.where(low, pltpu.roll(even[0:64], 64, 1), odd[0:64])
        pos = jnp.where(low8, even[64:72], pltpu.roll(odd[64:72], 64, 1))
        oe, oo = OFFSETS[2 * p], OFFSETS[2 * p + 1]
        for c in range(3):
            if oe[c] != 0 or oo[c] != 0:
                pos = jnp.where(sub8 == 3 + c, jnp.where(low8, float(oe[c]), float(oo[c])), pos)
        place(g, slice(at, at + 128), jnp.concatenate([top, bottom, pos], axis=0))
    tab[...] = tab32[...].astype(BF16)

    def slot_row(step):
        s = jnp.concatenate(
            [slots_ref[pl.ds(PER * step + j, 1), :] for j in range(PER)], axis=1
        )
        return jnp.broadcast_to(s, (8, NE))

    def harmonic(x, y, z, dsq):
        third = dsq * (1.0 / 3.0)
        return [None, x, y, z, x * y, y * z, x * z, x * x - third, y * y - third]

    degree = [0, 1, 1, 1, 2, 2, 2, 2, 2]

    def act(pre):
        sig = 0.5 + 0.5 * jnp.tanh(0.5 * pre)
        out = pre * sig
        return out, sig + out * (1.0 - sig)

    def gather(step, lanes, _):
        s = slot_row(step)
        group = s >> 8
        hi = s & 255
        valid = jnp.where(group < GROUPS, 1.0, 0.0)
        sub = iota((8, NE), 0)
        onehot = jnp.concatenate(
            [jnp.where(sub + 8 * t == hi, 1.0, 0.0) for t in range(32)], axis=0
        ).astype(BF16)
        hot_s[:, lanes] = onehot
        got = mm(tab[...], onehot)
        masks = [group == k for k in range(GROUPS)]
        for t in range(17):
            v = jnp.zeros((8, NE), F32)
            for k in range(GROUPS):
                at = 8 * (GROUPS * t + k)
                v = jnp.where(masks[k], got[at : at + 8], v)
            if t < 16:
                h_s[8 * t : 8 * t + 8, lanes] = v
        return v, valid

    def radial_one(step, lanes, given):
        pos, valid = given
        sub = iota((8, NE), 0)
        rel = []
        for c in range(3):
            sent = pos[c : c + 1] - pos[3 + c : 4 + c]
            rel.append(jnp.broadcast_to(sent, (8, NE)) - myc[8 * c : 8 * c + 8, :])
        x, y, z = rel
        dsq = x * x + y * y + z * z
        e0 = jnp.maximum(0.0, 1.0 - dsq * 0.25) * valid
        basis = jnp.exp(-dsq * beta)
        packed = jnp.zeros((8, NE), F32)
        for j, v in enumerate((x, y, z, dsq, e0 * e0, e0)):
            packed = jnp.where(sub == j, v, packed)
        row_s[:, lanes] = packed
        bas_s[:, lanes] = basis
        return mm(w1f[...], value_stack(basis))

    def radial_two(step, lanes, pre):
        h1, d1 = act(pre)
        d1_s[:, lanes] = d1
        return mm(w2f[...], value_stack(h1))

    def radial_three(step, lanes, pre):
        h2, d2 = act(pre)
        d2_s[:, lanes] = d2
        rad_s[:, lanes] = mm(w3f[...], value_stack(h2))

    def row_values(lanes):
        rows = row_s[:, lanes]
        return [jnp.broadcast_to(rows[j : j + 1], (8, NE)) for j in range(6)]

    def gather_sums(step, lanes, _):
        x, y, z, dsq, env, _ = row_values(lanes)
        ys = harmonic(x, y, z, dsq)
        for t in range(16):
            he = h_s[8 * t : 8 * t + 8, lanes] * env
            ds = [he * rad_s[128 * l + 8 * t : 128 * l + 8 * t + 8, lanes] for l in range(3)]
            for m in range(9):
                msg = ds[degree[m]] if m == 0 else ds[degree[m]] * ys[m]
                at = 128 * m + 8 * t
                acc[at : at + 8, :] += fold(msg)

    def staged(stages, step):
        lanes = pl.ds(pl.multiple_of(step * NE, NE), NE)
        held = None
        for stage in stages:
            held = stage(step, lanes, held)
        return held

    def fwd(step, carry):
        staged([gather, radial_one, radial_two, radial_three, gather_sums], step)
        return carry

    lax.fori_loop(0, STEPS, fwd, 0)

    def node(m):
        return acc[128 * m : 128 * m + 128, :] * 0.125

    a0, vx, vy, vz, xy, yz, xz, xx, yy = [node(m) for m in range(9)]
    zz = -xx - yy
    n1 = vx * vx + vy * vy + vz * vz
    n2 = xx * xx + yy * yy + zz * zz + 2.0 * (xy * xy + yz * yz + xz * xz)
    cx = xx * vx + xy * vy + xz * vz
    cy = xy * vx + yy * vy + yz * vz
    cz = xz * vx + yz * vy + zz * vz
    cub = cx * vx + cy * vy + cz * vz
    inv = jnp.concatenate([a0, n1, n2, a0 * n1, cub], axis=0)
    pre = mm_high(mix_ref[...].T, inv)
    sig = 0.5 + 0.5 * jnp.tanh(0.5 * pre)
    hid = pre * sig
    kinds = species_ref[pl.ds(quarter, 1), :]
    kind_hot = jnp.where(iota((128, 128), 0) == kinds, 1.0, 0.0)
    per_kind = mm_high(sp_s[...].T, kind_hot)
    energy_ref[...] = jnp.sum(hid * per_kind, axis=0, keepdims=True)
    dpre = per_kind * (sig + hid * (1.0 - sig))
    dinv = mm_high(mix_ref[...], dpre) * 0.125
    g0, g1, g2, g3, g4 = [dinv[128 * j : 128 * j + 128] for j in range(5)]
    w = 2.0 * (g1 + g3 * a0)
    c2 = 2.0 * g4
    acc[0:128, :] = g0 + g3 * n1
    acc[128:256, :] = w * vx + c2 * cx
    acc[256:384, :] = w * vy + c2 * cy
    acc[384:512, :] = w * vz + c2 * cz
    acc[512:640, :] = 4.0 * xy * g2 + c2 * vx * vy
    acc[640:768, :] = 4.0 * yz * g2 + c2 * vy * vz
    acc[768:896, :] = 4.0 * xz * g2 + c2 * vx * vz
    acc[896:1024, :] = 2.0 * g2 * (xx - zz) + g4 * (vx * vx - vz * vz)
    acc[1024:1152, :] = 2.0 * g2 * (yy - zz) + g4 * (vy * vy - vz * vz)

    def edge_grads(step, lanes, _):
        x, y, z, dsq, env, _ = row_values(lanes)
        ys = harmonic(x, y, z, dsq)
        denv = jnp.zeros((8, NE), F32)
        dys = [jnp.zeros((8, NE), F32) for _ in range(9)]
        dhs, drs = [], [[], [], []]
        for t in range(16):
            da = []
            for m in range(9):
                v = acc[128 * m + 8 * t : 128 * m + 8 * t + 8, :]
                da.append(jnp.concatenate([v] * PER, axis=1))
            t0 = da[0]
            t1 = x * da[1] + y * da[2] + z * da[3]
            t2 = ys[4] * da[4]
            for m in range(5, 9):
                t2 = t2 + ys[m] * da[m]
            ts = [t0, t1, t2]
            rs = [rad_s[128 * l + 8 * t : 128 * l + 8 * t + 8, lanes] for l in range(3)]
            u = rs[0] * t0 + rs[1] * t1 + rs[2] * t2
            h = h_s[8 * t : 8 * t + 8, lanes]
            he = h * env
            denv = denv + h * u
            dhs.append(env * u)
            for l in range(3):
                drs[l].append(he * ts[l])
            d1, d2 = he * rs[1], he * rs[2]
            for m in range(1, 9):
                dys[m] = dys[m] + (d1 if m < 4 else d2) * da[m]
        drad = jnp.concatenate(drs[0] + drs[1] + drs[2], axis=0).astype(BF16)
        both = mm(w3b[...], drad)
        dh_s[0:128, lanes] = jnp.concatenate(dhs, axis=0).astype(BF16)
        return denv, dys, both

    def radial_back_two(step, lanes, given):
        denv, dys, both = given
        dp2 = (both[0:64] + both[64:128]) * d2_s[:, lanes]
        return denv, dys, mm(w2b[...], value_stack(dp2))

    def radial_back_one(step, lanes, given):
        denv, dys, dh1 = given
        return denv, dys, mm(w1b[...], value_stack(dh1 * d1_s[:, lanes]))

    def position_grads(step, lanes, given):
        denv, dys, dbas = given

        def total(v):
            return jnp.broadcast_to(jnp.sum(v, axis=0, keepdims=True), (8, NE))

        x, y, z, _, _, e0 = row_values(lanes)
        denv = total(denv)
        dys = [None] + [total(v) for v in dys[1:]]
        ddsq = (
            -total(dbas * bas_s[:, lanes] * beta)
            - 0.5 * e0 * denv
            - (dys[7] + dys[8]) * (1.0 / 3.0)
        )
        two = 2.0 * ddsq
        dx = dys[1] + y * dys[4] + z * dys[6] + 2.0 * x * dys[7] + x * two
        dy = dys[2] + x * dys[4] + z * dys[5] + 2.0 * y * dys[8] + y * two
        dz = dys[3] + y * dys[5] + x * dys[6] + z * two
        sub = iota((8, NE), 0)
        return jnp.where(sub == 0, dx, jnp.where(sub == 1, dy, jnp.where(sub == 2, dz, 0.0)))

    def masked(step, lanes, groups):
        group = slot_row(step) >> 8
        group16 = jnp.concatenate([group, group], axis=0)
        lefts = []
        for k in groups:
            mask = jnp.where(group16 == k, 1.0, 0.0).astype(BF16)
            lefts.extend(dh_s[16 * t : 16 * t + 16, lanes] * mask for t in range(GROWS // 16))
        return jnp.concatenate(lefts, axis=0)

    def spread(step, lanes, drel):
        drel_hi = drel.astype(BF16).astype(F32)
        dh_s[128:144, lanes] = jnp.concatenate([drel_hi, drel - drel_hi], axis=0).astype(BF16)
        scat[2 * GROWS :, :] += mm_nt(masked(step, lanes, range(2, GROUPS)), hot_s[:, lanes])
        return fold(drel)

    def bwd(step, down):
        stages = [edge_grads, radial_back_two, radial_back_one, position_grads, spread]
        return down + staged(stages, step)

    down = lax.fori_loop(0, STEPS, bwd, jnp.zeros((8, 128), F32))

    for p in range(PAIRS):
        g, at = 2 + p // 2, 128 * (p % 2)
        top = scat[GROWS * g : GROWS * g + 64, at : at + 128]
        bottom = scat[GROWS * g + 64 : GROWS * g + 128, at : at + 128]
        pos = (
            scat[GROWS * g + 128 : GROWS * g + 136, at : at + 128]
            + scat[GROWS * g + 136 : GROWS * g + 144, at : at + 128]
        )
        pos_hi = pos.astype(BF16).astype(F32)
        pos = jnp.concatenate([pos_hi, pos - pos_hi], axis=0)
        even = jnp.where(low, top, pltpu.roll(bottom, 64, 1))
        odd = jnp.where(low, pltpu.roll(top, 64, 1), bottom)
        gblocks_ref[0, p, 0:64, :] = even.astype(BF16)
        gblocks_ref[1, p, 0:64, :] = odd.astype(BF16)
        gblocks_ref[0, p, 64:80, :] = jnp.where(low16, pos, 0.0).astype(BF16)
        gblocks_ref[1, p, 64:80, :] = jnp.where(low16, pltpu.roll(pos, 64, 1), 0.0).astype(BF16)


    pool = pltpu.make_async_remote_copy(
        src_ref=gblocks_ref.at[1 - core],
        dst_ref=matebuf,
        send_sem=back_send_sem.at[PAIRS + QUART - 1],
        recv_sem=back_recv_sem.at[PAIRS + QUART - 1],
        device_id=(me, mate),
        device_id_type=MESH,
    )
    pool.start()

    def own_spread(step, carry):
        lanes = pl.ds(pl.multiple_of(step * NE, NE), NE)
        scat[0 : 2 * GROWS, :] += mm_nt(masked(step, lanes, range(2)), hot_s[:, lanes])
        return carry

    lax.fori_loop(0, STEPS // 2, own_spread, 0)
    pool.wait_recv()
    backs = []
    for i in range(PAIRS):
        backblk[i] = (gblocks_ref[core, i].astype(F32) + matebuf[i].astype(F32)).astype(BF16)
        copy = pltpu.make_async_remote_copy(
            src_ref=backblk.at[i],
            dst_ref=landed.at[i],
            send_sem=back_send_sem.at[i],
            recv_sem=back_recv_sem.at[i],
            device_id=offset_device(dom_size, i, core, -1),
            device_id_type=MESH,
        )
        copy.start()
        backs.append(copy)

    lax.fori_loop(STEPS // 2, STEPS, own_spread, 0)
    for g in range(2):
        span = slice(256 * g, 256 * g + 256)
        gown_ref[0:128, span] = scat[GROWS * g : GROWS * g + 128, :]
        gown_ref[128:136, span] = (
            scat[GROWS * g + 128 : GROWS * g + 136, :] + scat[GROWS * g + 136 : GROWS * g + 144, :]
        )
    gown_ref[128:136, mine] = gown_ref[128:136, mine] - down

    total = jnp.zeros((GROWS, ATOMS), F32)
    for i in range(0, PAIRS, 2):
        even = landed_block(backs, landed, i)
        odd = landed_block(backs, landed, i + 1) if i + 1 < PAIRS else jnp.zeros((BLK, 128), F32)
        top = jnp.where(low, even[0:64], pltpu.roll(odd[0:64], 64, 1))
        bottom = jnp.where(low, pltpu.roll(even[0:64], 64, 1), odd[0:64])
        pos = jnp.where(low16, even[64:80], pltpu.roll(odd[64:80], 64, 1))
        left = jnp.concatenate([top, bottom, pos], axis=0).astype(BF16)
        onehot = jnp.where(iota((ATOMS, 128), 0) == map_rows(gmap_ref, core, i), 1.0, 0.0)
        total = total + mm_nt(left, onehot.astype(BF16))
    feat = total[0:128] + gown_ref[0:128, :]
    pos = total[128:136] + total[136:144] + gown_ref[128:136, :]
    for j in range(QUART):
        span = slice(128 * j, 128 * j + 128)
        part[j, 0:128, :] = feat[:, span]
        part[j, 128:136, :] = pos[:, span]

    sums = []
    for j in range(1, QUART):
        peer = lax.rem(quarter + j, QUART)
        copy = pltpu.make_async_remote_copy(
            src_ref=part.at[peer],
            dst_ref=heard.at[j - 1],
            send_sem=back_send_sem.at[PAIRS + j - 1],
            recv_sem=back_recv_sem.at[PAIRS + j - 1],
            device_id=(me, peer),
            device_id_type=MESH,
        )
        copy.start()
        sums.append(copy)
    got = part[quarter]
    for j, copy in enumerate(sums):
        copy.wait_recv()
        got = got + heard[j]
    grad_ref[...] = got
    for copy in backs + sums + [pool]:
        copy.wait_send()


def compute_call(*operands):
    sds = jax.ShapeDtypeStruct
    edge_total = OWN * RANKS
    return pl.pallas_call(
        compute_kernel,
        out_shape=(sds((1, OWN), F32), sds((2, PAIRS, BLK, 128), BF16), sds((136, ATOMS), F32)),
        in_specs=[VMEM_SPEC] * 10,
        out_specs=(VMEM_SPEC,) * 3,
        scratch_shapes=[
            pltpu.VMEM((TROWS, 256), BF16),
            pltpu.VMEM((TROWS, 256), F32),
            pltpu.VMEM((CH, edge_total), BF16),
            pltpu.VMEM((256, edge_total), BF16),
            pltpu.VMEM((9 * CH, OWN), F32),
            pltpu.VMEM((3 * CH, edge_total), F32),
            pltpu.VMEM((CH, edge_total), F32),
            pltpu.VMEM((64, edge_total), F32),
            pltpu.VMEM((64, edge_total), F32),
            pltpu.VMEM((8, edge_total), F32),
            pltpu.VMEM((8, edge_total), F32),
            pltpu.VMEM((GROUPS * GROWS, 256), F32),
            pltpu.VMEM((128, 128), F32),
            pltpu.VMEM((64, 24), BF16),
            pltpu.VMEM((64, 192), BF16),
            pltpu.VMEM((384, 192), BF16),
            pltpu.VMEM((8, 192), BF16),
            pltpu.VMEM((64, 192), BF16),
            pltpu.VMEM((128, 384), BF16),
            pltpu.VMEM((24, NE), F32),
        ],
        compiler_params=pltpu.CompilerParams(vmem_limit_bytes=LIMIT),
        name="compute",
    )(*operands)


def finish_kernel(energy_ref, grad_ref, wup_ref, energy_out, force_out, fgrad_out):
    energy_out[...] = energy_ref[...]
    force_out[...] = -grad_ref[128:131, :]
    fgrad_out[...] = lax.dot_general(
        grad_ref[0:128, :].T,
        wup_ref[...].astype(F32),
        (((1,), (1,)), ((), ())),
        precision=HIGH,
        preferred_element_type=F32,
    )


def interaction_call(dom_size, *operands):
    sds = jax.ShapeDtypeStruct
    edges = QUART * EDGE_ROWS
    edge_total = OWN * RANKS
    return pl.pallas_call(
        lambda *refs: interaction_kernel(dom_size, *refs),
        out_shape=(sds((1, OWN), F32), sds((136, OWN), F32)),
        in_specs=[VMEM_SPEC] * 6 + [pl.BlockSpec(memory_space=pltpu.SMEM)] + [VMEM_SPEC] * 6,
        out_specs=(VMEM_SPEC,) * 2,
        scratch_shapes=[
            pltpu.VMEM((RANKS, OWN), I32),
            pltpu.VMEM((2, PAIRS, BLK, 128), BF16),
            pltpu.VMEM((CH, ATOMS), BF16),
            pltpu.VMEM((2, PAIRS, BLK, 128), BF16),
            pltpu.VMEM((136, ATOMS), F32),
            pltpu.VMEM((PAIRS, BLK, 128), BF16),
            pltpu.VMEM((QUART, EDGE_ROWS, 128), I32),
            pltpu.VMEM((edges, 128), F32),
            pltpu.VMEM((edges, 128), F32),
            pltpu.VMEM((edges, 128), F32),
            pltpu.VMEM((256, 384), BF16),
            pltpu.VMEM((TROWS, 256), BF16),
            pltpu.VMEM((TROWS, 256), F32),
            pltpu.VMEM((GROWS, edge_total), BF16),
            pltpu.VMEM((256, edge_total), BF16),
            pltpu.VMEM((9 * CH, OWN), F32),
            pltpu.VMEM((3 * CH, edge_total), F32),
            pltpu.VMEM((CH, edge_total), F32),
            pltpu.VMEM((64, edge_total), F32),
            pltpu.VMEM((64, edge_total), F32),
            pltpu.VMEM((8, edge_total), F32),
            pltpu.VMEM((8, edge_total), F32),
            pltpu.VMEM((GROUPS * GROWS, 256), F32),
            pltpu.VMEM((128, 128), F32),
            pltpu.VMEM((64, 24), BF16),
            pltpu.VMEM((64, 192), BF16),
            pltpu.VMEM((384, 192), BF16),
            pltpu.VMEM((8, 192), BF16),
            pltpu.VMEM((64, 192), BF16),
            pltpu.VMEM((128, 384), BF16),
            pltpu.VMEM((24, NE), F32),
            pltpu.VMEM((PAIRS, BLK, 128), BF16),
            pltpu.VMEM((PAIRS, BLK, 128), BF16),
            pltpu.VMEM((PAIRS, BLK, 128), BF16),
            pltpu.VMEM((QUART, 136, 128), F32),
            pltpu.VMEM((QUART - 1, 136, 128), F32),
            pltpu.SemaphoreType.DMA((PAIRS + QUART,)),
            pltpu.SemaphoreType.DMA((PAIRS + QUART,)),
            pltpu.SemaphoreType.DMA((PAIRS + QUART,)),
            pltpu.SemaphoreType.DMA((PAIRS + QUART,)),
        ],
        compiler_params=pltpu.CompilerParams(
            collective_id=0, has_side_effects=True, vmem_limit_bytes=LIMIT
        ),
        name="interaction",
    )(*operands)


def on_device(
    dom_size, coordinates, features, species, ghost_map, edge_sender, edge_receiver, edge_count,
    w_up, radial_one, radial_two, radial_three, read_mix, species_out,
):
    sds = jax.ShapeDtypeStruct
    energy, grad = interaction_call(
        dom_size, features, w_up, coordinates, ghost_map,
        edge_sender.reshape(EDGE_ROWS, 128), edge_receiver.reshape(EDGE_ROWS, 128), edge_count,
        species.reshape(QUART, OWN), radial_one, radial_two, radial_three, read_mix, species_out,
    )
    energy, forces, feature_grad = pl.pallas_call(
        finish_kernel,
        out_shape=(sds((1, OWN), F32), sds((3, OWN), F32), sds((OWN, CH), F32)),
        in_specs=[VMEM_SPEC] * 3,
        out_specs=(VMEM_SPEC,) * 3,
        name="finish",
    )(energy, grad, w_up)
    return energy.reshape(OWN), forces, feature_grad


def solution(mesh):
    dom_size = mesh.shape["dom"]
    return jax.shard_map(
        lambda *args: on_device(dom_size, *args),
        mesh=mesh,
        in_specs=(
            P(None, "dom"),
            P("dom", None),
            P("dom"),
            P("dom", None),
            P(("dom", "edge")),
            P(("dom", "edge")),
            P("dom"),
            P(),
            P(),
            P(),
            P(),
            P(),
            P(),
        ),
        out_specs=(P(("dom", "edge")), P(None, ("dom", "edge")), P(("dom", "edge"), None)),
        check_vma=False,
    )
```

```python
import jax
import jax.numpy as jnp
from jax import lax
from jax.experimental import pallas as pl
from jax.experimental.pallas import tpu as pltpu
from jax.sharding import PartitionSpec as P

F32, BF16, I32 = jnp.float32, jnp.bfloat16, jnp.int32
HIGH = lax.Precision.HIGHEST
MESH = pl.DeviceIdType.MESH
VMEM_SPEC = pl.BlockSpec(memory_space=pltpu.VMEM)

CH = 128
ATOMS = 512
OWN = 128
RANKS = 64
SLOT = 64
NOFF = 26
PAIRS = NOFF // 2
QUART = 4
EDGE_ROWS = 64
GROUPS = 9
GROWS = 144
TROWS = 1232
PER = 16
NE = PER * OWN
STEPS = OWN * RANKS // NE
BLK = 80
SENTINEL = 4095
LIMIT = 56 * 1024 * 1024

OFFSETS = [
    (a, b, c)
    for a in (-1, 0, 1)
    for b in (-1, 0, 1)
    for c in (-1, 0, 1)
    if (a, b, c) != (0, 0, 0)
]


SEND_ORDER = sorted(range(PAIRS), key=lambda i: -abs(2 * i - PAIRS + 1))


def shifts(count):
    side = 1
    while side * side * side < count:
        side += 1
    return [o[0] * side * side + o[1] * side + o[2] for o in OFFSETS]


def mm(a, b):
    return lax.dot_general(a, b, (((1,), (0,)), ((), ())), preferred_element_type=F32)


def mm_nt(a, b):
    return lax.dot_general(a, b, (((1,), (1,)), ((), ())), preferred_element_type=F32)


def mm_high(a, b):
    return lax.dot_general(
        a, b, (((1,), (0,)), ((), ())), precision=HIGH, preferred_element_type=F32
    )


def split(x):
    hi = x.astype(BF16)
    return hi, (x - hi.astype(F32)).astype(BF16)


def weight_stack(w):
    hi, lo = split(w)
    return jnp.concatenate([hi, hi, lo], axis=1)


def value_stack(x):
    hi, lo = split(x)
    return jnp.concatenate([hi, lo, hi], axis=0)


def iota(shape, dim):
    return lax.broadcasted_iota(I32, shape, dim)


def fold(x):
    parts = [x[:, 128 * j : 128 * (j + 1)] for j in range(x.shape[1] // 128)]
    while len(parts) > 1:
        parts = [parts[j] + parts[j + 1] for j in range(0, len(parts), 2)]
    return parts[0]


def map_rows(gmap_ref, core, i):
    other = min(i + 1, PAIRS - 1)
    return jnp.concatenate(
        [gmap_ref[pl.ds(2 * i + core, 1), :], gmap_ref[pl.ds(2 * other + core, 1), :]], axis=1
    )


def offset_device(dom_size, i, core, sign):
    me, quarter = lax.axis_index("dom"), lax.axis_index("edge")
    even, odd = [(shifts(dom_size)[2 * i + j] * sign) % dom_size for j in (0, 1)]
    swap_even, swap_odd = [int(OFFSETS[2 * i + j][2] != 0) for j in (0, 1)]
    there = lax.rem(me + even + core * (odd - even), dom_size)
    swap = swap_even + core * (swap_odd - swap_even)
    return there, lax.rem(quarter + 2 * swap, QUART)


def greet(dom_size):
    barrier = pltpu.get_barrier_semaphore()
    quarter = lax.axis_index("edge")
    me = lax.axis_index("dom")
    core = lax.rem(quarter, 2)
    for i in range(PAIRS):
        for sign in (1, -1):
            there = offset_device(dom_size, i, core, sign)
            pl.semaphore_signal(barrier, inc=1, device_id=there, device_id_type=MESH)
    for j in range(1, QUART):
        peer = lax.rem(quarter + j, QUART)
        pl.semaphore_signal(barrier, inc=1, device_id=(me, peer), device_id_type=MESH)
    return barrier


def landed_block(copies, landed, i):
    copies[i].wait_recv()
    return landed[i].astype(F32)


def interaction_kernel(
    dom_size,
    feat_ref, wup_ref, coord_ref, gmap_ref, snd_ref, rcv_ref, cnt_ref, species_ref,
    w1_ref, w2_ref, w3_ref, mix_ref, sp_ref,
    energy_ref, grad_ref,
    slots_ref, blocks_ref, own_ref, gblocks_ref, gown_ref,
    sendblk, epack, tri_s,
    tab, tab32, dh_s, hot_s, acc, rad_s, h_s, d1_s, d2_s, bas_s, row_s, scat, sp_s,
    w1f, w2f, w3f, w1b, w2b, w3b, myc, mix_t, kind_s,
    matebuf, backblk, landed, part, heard, send_sem, recv_sem, back_send_sem, back_recv_sem,
):
    me = lax.axis_index("dom")
    quarter = lax.axis_index("edge")
    core = lax.rem(quarter, 2)
    mate = quarter + 1 - 2 * core
    barrier = greet(dom_size)

    first = quarter * (EDGE_ROWS * 128)
    index = first + iota((EDGE_ROWS, 128), 0) * 128 + iota((EDGE_ROWS, 128), 1)
    sender = jnp.where(index < cnt_ref[0], snd_ref[...], SENTINEL)
    epack[quarter] = sender + rcv_ref[...] * 65536

    hprime = mm(feat_ref[...], wup_ref[...]).astype(BF16)
    h_t = hprime.astype(F32).T.astype(BF16)
    own_ref[...] = h_t
    coords = jnp.concatenate(
        [coord_ref[...].astype(F32), jnp.zeros((13, ATOMS), F32)], axis=0
    ).astype(BF16)
    ext = jnp.concatenate([h_t, coords], axis=0)

    low = iota((64, 128), 1) < 64
    low16 = iota((16, 128), 1) < 64
    low8 = iota((8, 128), 1) < 64
    sub8 = iota((8, 128), 0)
    for i in range(0, PAIRS, 2):
        onehot = jnp.where(iota((ATOMS, 128), 0) == map_rows(gmap_ref, core, i), 1.0, 0.0)
        picked = mm(ext, onehot.astype(BF16))
        top, bottom, pos = picked[0:64], picked[64:128], picked[128:144]
        sendblk[i, 0:64, :] = jnp.where(low, top, pltpu.roll(bottom, 64, 1)).astype(BF16)
        sendblk[i, 64:80, :] = pos.astype(BF16)
        if i + 1 < PAIRS:
            sendblk[i + 1, 0:64, :] = jnp.where(low, pltpu.roll(top, 64, 1), bottom).astype(BF16)
            sendblk[i + 1, 64:80, :] = pltpu.roll(pos, 64, 1).astype(BF16)

    pl.semaphore_wait(barrier, NOFF + QUART - 1)

    copies = []
    for j in range(1, QUART):
        peer = lax.rem(quarter + j, QUART)
        copy = pltpu.make_async_remote_copy(
            src_ref=epack.at[quarter],
            dst_ref=epack.at[quarter],
            send_sem=send_sem.at[PAIRS + j - 1],
            recv_sem=recv_sem.at[PAIRS + j - 1],
            device_id=(me, peer),
            device_id_type=MESH,
        )
        copy.start()
        copies.append(copy)

    ghosts = [None] * PAIRS
    for j in SEND_ORDER:
        copy = pltpu.make_async_remote_copy(
            src_ref=sendblk.at[j],
            dst_ref=blocks_ref.at[core, j],
            send_sem=send_sem.at[j],
            recv_sem=recv_sem.at[j],
            device_id=offset_device(dom_size, j, core, 1),
            device_id_type=MESH,
        )
        copy.start()
        ghosts[j] = copy

    coords = coord_ref[...].astype(F32)
    coords8 = jnp.concatenate([coords, jnp.zeros((5, ATOMS), F32)], axis=0)
    def place(g, lanes, rows):
        for t in range(17):
            tab32[8 * (GROUPS * t + g) : 8 * (GROUPS * t + g) + 8, lanes] = rows[8 * t : 8 * t + 8]

    for g in range(2):
        span = slice(256 * g, 256 * g + 256)
        place(g, slice(0, 256), jnp.concatenate([own_ref[:, span].astype(F32), coords8[:, span]], axis=0))
    place(8, slice(0, 256), jnp.zeros((136, 256), F32))
    tab32[8 * GROUPS * 17 :, :] = jnp.zeros((TROWS - 8 * GROUPS * 17, 256), F32)
    w1f[...] = weight_stack(w1_ref[...].T)
    w2f[...] = weight_stack(w2_ref[...].T)
    w3f[...] = weight_stack(w3_ref[...].T)
    w1b[...] = weight_stack(w1_ref[...])
    w2b[...] = weight_stack(w2_ref[...])
    hi, lo = split(w3_ref[...])
    w3b[...] = jnp.concatenate([hi, lo], axis=0)

    acc[...] = jnp.zeros(acc.shape, F32)
    scat[...] = jnp.zeros(scat.shape, F32)
    mine = pl.ds(pl.multiple_of(quarter * OWN, OWN), OWN)
    my_coords = coord_ref[:, mine].astype(F32)
    for c in range(3):
        mc = jnp.broadcast_to(my_coords[c : c + 1], (8, 128))
        myc[8 * c : 8 * c + 8, :] = jnp.concatenate([mc] * PER, axis=1)

    beta = jnp.zeros((8, NE), F32)
    for n in range(8):
        beta = jnp.where(iota((8, NE), 0) == n, 0.4 * 15.0 ** (n / 7.0), beta)

    sp_s[...] = jnp.zeros((128, 128), F32)
    sp_s[0:89, :] = sp_ref[...]
    kinds = species_ref[pl.ds(quarter, 1), :]
    kind_hot = jnp.where(iota((128, 128), 0) == kinds, 1.0, 0.0)
    kind_s[...] = mm_high(sp_s[...].T, kind_hot)
    mix_t[...] = mix_ref[...].T

    tri_s[:, 0:256] = jnp.where(iota((256, 256), 0) < iota((256, 256), 1), 1.0, 0.0).astype(BF16)
    tri_s[:, 256:384] = jnp.ones((256, 128), BF16)

    atom = iota((OWN, 256), 0).astype(F32)
    rank_of = iota((RANKS, 256), 0).astype(F32)

    def sort_quarter(source, carry):
        base, total = carry
        packed = epack[source]
        local = (packed >> 16) - quarter * OWN
        inside = (local >= 0) & (local < OWN)
        li8 = jnp.where(inside, local, 255).astype(F32)
        value = packed & 65535
        g8 = (value >> 8).astype(F32)
        hi8 = (value & 255).astype(F32)

        def lane_row(x, b):
            return jnp.concatenate([x[2 * b : 2 * b + 1], x[2 * b + 1 : 2 * b + 2]], axis=1)

        hots = [jnp.where(atom == lane_row(li8, b), 1.0, 0.0) for b in range(EDGE_ROWS // 2)]
        hots16 = [hot.astype(BF16) for hot in hots]
        counts = mm(jnp.concatenate(hots16, axis=0), tri_s[...])
        lefts = []
        for b in range(EDGE_ROWS // 2):
            block = counts[OWN * b : OWN * (b + 1)]
            before = block[:, 0:256] + jnp.concatenate([base, base], axis=1)
            base = base + block[:, 256:384]
            rank = jnp.sum(before * hots[b], axis=0, keepdims=True)
            here = rank_of == rank
            lefts.append(
                jnp.concatenate(
                    [
                        jnp.where(here, lane_row(g8, b), 0.0).astype(BF16),
                        jnp.where(here, lane_row(hi8, b), 0.0).astype(BF16),
                    ],
                    axis=0,
                )
            )
        total = total + mm_nt(jnp.concatenate(lefts, axis=1), jnp.concatenate(hots16, axis=1))
        return base, total

    zero = jnp.zeros((OWN, 128), F32)
    state = sort_quarter(quarter, (zero, zero))
    for j in (1, 2):
        copies[j - 1].wait_recv()
        state = sort_quarter(lax.rem(quarter + QUART - j, QUART), state)
    for copy in ghosts:
        copy.wait_recv()
    share = pltpu.make_async_remote_copy(
        src_ref=blocks_ref.at[core],
        dst_ref=blocks_ref.at[core],
        send_sem=send_sem.at[PAIRS + QUART - 1],
        recv_sem=recv_sem.at[PAIRS + QUART - 1],
        device_id=(me, mate),
        device_id_type=MESH,
    )
    share.start()
    copies[2].wait_recv()
    _, total = sort_quarter(lax.rem(quarter + QUART - 3, QUART), state)
    slots_ref[...] = (total[0:64] * 256.0 + total[64:128]).astype(I32)
    share.wait_recv()
    for copy in copies + ghosts + [share]:
        copy.wait_send()


    for p in range(PAIRS):
        g, at = 2 + p // 2, 128 * (p % 2)
        even = blocks_ref[0, p].astype(F32)
        odd = blocks_ref[1, p].astype(F32)
        top = jnp.where(low, even[0:64], pltpu.roll(odd[0:64], 64, 1))
        bottom = jnp.where(low, pltpu.roll(even[0:64], 64, 1), odd[0:64])
        pos = jnp.where(low8, even[64:72], pltpu.roll(odd[64:72], 64, 1))
        oe, oo = OFFSETS[2 * p], OFFSETS[2 * p + 1]
        for c in range(3):
            if oe[c] != 0 or oo[c] != 0:
                pos = jnp.where(sub8 == 3 + c, jnp.where(low8, float(oe[c]), float(oo[c])), pos)
        place(g, slice(at, at + 128), jnp.concatenate([top, bottom, pos], axis=0))
    tab[...] = tab32[...].astype(BF16)

    def slot_row(step):
        s = jnp.concatenate(
            [slots_ref[pl.ds(PER * step + j, 1), :] for j in range(PER)], axis=1
        )
        return jnp.broadcast_to(s, (8, NE))

    def harmonic(x, y, z, dsq):
        third = dsq * (1.0 / 3.0)
        return [None, x, y, z, x * y, y * z, x * z, x * x - third, y * y - third]

    degree = [0, 1, 1, 1, 2, 2, 2, 2, 2]

    def act(pre):
        sig = 0.5 + 0.5 * jnp.tanh(0.5 * pre)
        out = pre * sig
        return out, sig + out * (1.0 - sig)

    def gather(step, lanes, _):
        s = slot_row(step)
        group = s >> 8
        hi = s & 255
        valid = jnp.where(group < GROUPS, 1.0, 0.0)
        sub = iota((8, NE), 0)
        onehot = jnp.concatenate(
            [jnp.where(sub + 8 * t == hi, 1.0, 0.0) for t in range(32)], axis=0
        ).astype(BF16)
        hot_s[:, lanes] = onehot
        got = mm(tab[...], onehot)
        masks = [group == k for k in range(GROUPS)]
        for t in range(17):
            v = jnp.zeros((8, NE), F32)
            for k in range(GROUPS):
                at = 8 * (GROUPS * t + k)
                v = jnp.where(masks[k], got[at : at + 8], v)
            if t < 16:
                h_s[8 * t : 8 * t + 8, lanes] = v
        return v, valid

    def radial_one(step, lanes, given):
        pos, valid = given
        sub = iota((8, NE), 0)
        rel = []
        for c in range(3):
            sent = pos[c : c + 1] - pos[3 + c : 4 + c]
            rel.append(jnp.broadcast_to(sent, (8, NE)) - myc[8 * c : 8 * c + 8, :])
        x, y, z = rel
        dsq = x * x + y * y + z * z
        e0 = jnp.maximum(0.0, 1.0 - dsq * 0.25) * valid
        basis = jnp.exp(-dsq * beta)
        packed = jnp.zeros((8, NE), F32)
        for j, v in enumerate((x, y, z, dsq, e0 * e0, e0)):
            packed = jnp.where(sub == j, v, packed)
        row_s[:, lanes] = packed
        bas_s[:, lanes] = basis
        return mm(w1f[...], value_stack(basis))

    def radial_two(step, lanes, pre):
        h1, d1 = act(pre)
        d1_s[:, lanes] = d1
        return mm(w2f[...], value_stack(h1))

    def radial_three(step, lanes, pre):
        h2, d2 = act(pre)
        d2_s[:, lanes] = d2
        rad_s[:, lanes] = mm(w3f[...], value_stack(h2))

    def row_values(lanes):
        rows = row_s[:, lanes]
        return [jnp.broadcast_to(rows[j : j + 1], (8, NE)) for j in range(6)]

    def gather_sums(step, lanes, _):
        x, y, z, dsq, env, _ = row_values(lanes)
        ys = harmonic(x, y, z, dsq)
        for t in range(16):
            he = h_s[8 * t : 8 * t + 8, lanes] * env
            ds = [he * rad_s[128 * l + 8 * t : 128 * l + 8 * t + 8, lanes] for l in range(3)]
            for m in range(9):
                msg = ds[degree[m]] if m == 0 else ds[degree[m]] * ys[m]
                at = 128 * m + 8 * t
                acc[at : at + 8, :] += fold(msg)

    def staged(stages, step):
        lanes = pl.ds(pl.multiple_of(step * NE, NE), NE)
        held = None
        for stage in stages:
            held = stage(step, lanes, held)
        return held

    def fwd(step, carry):
        staged([gather, radial_one, radial_two, radial_three, gather_sums], step)
        return carry

    lax.fori_loop(0, STEPS, fwd, 0)

    def node(m):
        return acc[128 * m : 128 * m + 128, :] * 0.125

    a0, vx, vy, vz, xy, yz, xz, xx, yy = [node(m) for m in range(9)]
    zz = -xx - yy
    n1 = vx * vx + vy * vy + vz * vz
    n2 = xx * xx + yy * yy + zz * zz + 2.0 * (xy * xy + yz * yz + xz * xz)
    cx = xx * vx + xy * vy + xz * vz
    cy = xy * vx + yy * vy + yz * vz
    cz = xz * vx + yz * vy + zz * vz
    cub = cx * vx + cy * vy + cz * vz
    inv = jnp.concatenate([a0, n1, n2, a0 * n1, cub], axis=0)
    pre = mm_high(mix_t[...], inv)
    sig = 0.5 + 0.5 * jnp.tanh(0.5 * pre)
    hid = pre * sig
    per_kind = kind_s[...]
    energy_ref[...] = jnp.sum(hid * per_kind, axis=0, keepdims=True)
    dpre = per_kind * (sig + hid * (1.0 - sig))
    dinv = mm_high(mix_ref[...], dpre) * 0.125
    g0, g1, g2, g3, g4 = [dinv[128 * j : 128 * j + 128] for j in range(5)]
    w = 2.0 * (g1 + g3 * a0)
    c2 = 2.0 * g4
    acc[0:128, :] = g0 + g3 * n1
    acc[128:256, :] = w * vx + c2 * cx
    acc[256:384, :] = w * vy + c2 * cy
    acc[384:512, :] = w * vz + c2 * cz
    acc[512:640, :] = 4.0 * xy * g2 + c2 * vx * vy
    acc[640:768, :] = 4.0 * yz * g2 + c2 * vy * vz
    acc[768:896, :] = 4.0 * xz * g2 + c2 * vx * vz
    acc[896:1024, :] = 2.0 * g2 * (xx - zz) + g4 * (vx * vx - vz * vz)
    acc[1024:1152, :] = 2.0 * g2 * (yy - zz) + g4 * (vy * vy - vz * vz)

    def edge_grads(step, lanes, _):
        x, y, z, dsq, env, _ = row_values(lanes)
        ys = harmonic(x, y, z, dsq)
        denv = jnp.zeros((8, NE), F32)
        dys = [jnp.zeros((8, NE), F32) for _ in range(9)]
        dhs, drs = [], [[], [], []]
        for t in range(16):
            da = []
            for m in range(9):
                v = acc[128 * m + 8 * t : 128 * m + 8 * t + 8, :]
                da.append(jnp.concatenate([v] * PER, axis=1))
            t0 = da[0]
            t1 = x * da[1] + y * da[2] + z * da[3]
            t2 = ys[4] * da[4]
            for m in range(5, 9):
                t2 = t2 + ys[m] * da[m]
            ts = [t0, t1, t2]
            rs = [rad_s[128 * l + 8 * t : 128 * l + 8 * t + 8, lanes] for l in range(3)]
            u = rs[0] * t0 + rs[1] * t1 + rs[2] * t2
            h = h_s[8 * t : 8 * t + 8, lanes]
            he = h * env
            denv = denv + h * u
            dhs.append(env * u)
            for l in range(3):
                drs[l].append(he * ts[l])
            d1, d2 = he * rs[1], he * rs[2]
            for m in range(1, 9):
                dys[m] = dys[m] + (d1 if m < 4 else d2) * da[m]
        drad = jnp.concatenate(drs[0] + drs[1] + drs[2], axis=0).astype(BF16)
        both = mm(w3b[...], drad)
        dh_s[0:128, lanes] = jnp.concatenate(dhs, axis=0).astype(BF16)
        return denv, dys, both

    def radial_back_two(step, lanes, given):
        denv, dys, both = given
        dp2 = (both[0:64] + both[64:128]) * d2_s[:, lanes]
        return denv, dys, mm(w2b[...], value_stack(dp2))

    def radial_back_one(step, lanes, given):
        denv, dys, dh1 = given
        return denv, dys, mm(w1b[...], value_stack(dh1 * d1_s[:, lanes]))

    def position_grads(step, lanes, given):
        denv, dys, dbas = given

        def total(v):
            return jnp.broadcast_to(jnp.sum(v, axis=0, keepdims=True), (8, NE))

        x, y, z, _, _, e0 = row_values(lanes)
        denv = total(denv)
        dys = [None] + [total(v) for v in dys[1:]]
        ddsq = (
            -total(dbas * bas_s[:, lanes] * beta)
            - 0.5 * e0 * denv
            - (dys[7] + dys[8]) * (1.0 / 3.0)
        )
        two = 2.0 * ddsq
        dx = dys[1] + y * dys[4] + z * dys[6] + 2.0 * x * dys[7] + x * two
        dy = dys[2] + x * dys[4] + z * dys[5] + 2.0 * y * dys[8] + y * two
        dz = dys[3] + y * dys[5] + x * dys[6] + z * two
        sub = iota((8, NE), 0)
        return jnp.where(sub == 0, dx, jnp.where(sub == 1, dy, jnp.where(sub == 2, dz, 0.0)))

    def masked(step, lanes, groups):
        group = slot_row(step) >> 8
        group16 = jnp.concatenate([group, group], axis=0)
        lefts = []
        for k in groups:
            mask = jnp.where(group16 == k, 1.0, 0.0).astype(BF16)
            lefts.extend(dh_s[16 * t : 16 * t + 16, lanes] * mask for t in range(GROWS // 16))
        return jnp.concatenate(lefts, axis=0)

    def spread(step, lanes, drel):
        drel_hi = drel.astype(BF16).astype(F32)
        dh_s[128:144, lanes] = jnp.concatenate([drel_hi, drel - drel_hi], axis=0).astype(BF16)
        scat[2 * GROWS :, :] += mm_nt(masked(step, lanes, range(2, GROUPS)), hot_s[:, lanes])
        return fold(drel)

    def bwd(step, down):
        stages = [edge_grads, radial_back_two, radial_back_one, position_grads, spread]
        return down + staged(stages, step)

    down = lax.fori_loop(0, STEPS, bwd, jnp.zeros((8, 128), F32))

    for p in range(PAIRS):
        g, at = 2 + p // 2, 128 * (p % 2)
        top = scat[GROWS * g : GROWS * g + 64, at : at + 128]
        bottom = scat[GROWS * g + 64 : GROWS * g + 128, at : at + 128]
        pos = (
            scat[GROWS * g + 128 : GROWS * g + 136, at : at + 128]
            + scat[GROWS * g + 136 : GROWS * g + 144, at : at + 128]
        )
        pos_hi = pos.astype(BF16).astype(F32)
        pos = jnp.concatenate([pos_hi, pos - pos_hi], axis=0)
        even = jnp.where(low, top, pltpu.roll(bottom, 64, 1))
        odd = jnp.where(low, pltpu.roll(top, 64, 1), bottom)
        gblocks_ref[0, p, 0:64, :] = even.astype(BF16)
        gblocks_ref[1, p, 0:64, :] = odd.astype(BF16)
        gblocks_ref[0, p, 64:80, :] = jnp.where(low16, pos, 0.0).astype(BF16)
        gblocks_ref[1, p, 64:80, :] = jnp.where(low16, pltpu.roll(pos, 64, 1), 0.0).astype(BF16)


    pool = pltpu.make_async_remote_copy(
        src_ref=gblocks_ref.at[1 - core],
        dst_ref=matebuf,
        send_sem=back_send_sem.at[PAIRS + QUART - 1],
        recv_sem=back_recv_sem.at[PAIRS + QUART - 1],
        device_id=(me, mate),
        device_id_type=MESH,
    )
    pool.start()

    def own_spread(step, carry):
        lanes = pl.ds(pl.multiple_of(step * NE, NE), NE)
        scat[0 : 2 * GROWS, :] += mm_nt(masked(step, lanes, range(2)), hot_s[:, lanes])
        return carry

    lax.fori_loop(0, STEPS // 2, own_spread, 0)
    pool.wait_recv()
    backs = [None] * PAIRS
    for i in SEND_ORDER:
        backblk[i] = (gblocks_ref[core, i].astype(F32) + matebuf[i].astype(F32)).astype(BF16)
        copy = pltpu.make_async_remote_copy(
            src_ref=backblk.at[i],
            dst_ref=landed.at[i],
            send_sem=back_send_sem.at[i],
            recv_sem=back_recv_sem.at[i],
            device_id=offset_device(dom_size, i, core, -1),
            device_id_type=MESH,
        )
        copy.start()
        backs[i] = copy

    lax.fori_loop(STEPS // 2, STEPS, own_spread, 0)
    for g in range(2):
        span = slice(256 * g, 256 * g + 256)
        gown_ref[0:128, span] = scat[GROWS * g : GROWS * g + 128, :]
        gown_ref[128:136, span] = (
            scat[GROWS * g + 128 : GROWS * g + 136, :] + scat[GROWS * g + 136 : GROWS * g + 144, :]
        )
    gown_ref[128:136, mine] = gown_ref[128:136, mine] - down

    total = jnp.zeros((GROWS, ATOMS), F32)
    for i in range(0, PAIRS, 2):
        even = landed_block(backs, landed, i)
        odd = landed_block(backs, landed, i + 1) if i + 1 < PAIRS else jnp.zeros((BLK, 128), F32)
        top = jnp.where(low, even[0:64], pltpu.roll(odd[0:64], 64, 1))
        bottom = jnp.where(low, pltpu.roll(even[0:64], 64, 1), odd[0:64])
        pos = jnp.where(low16, even[64:80], pltpu.roll(odd[64:80], 64, 1))
        left = jnp.concatenate([top, bottom, pos], axis=0).astype(BF16)
        onehot = jnp.where(iota((ATOMS, 128), 0) == map_rows(gmap_ref, core, i), 1.0, 0.0)
        total = total + mm_nt(left, onehot.astype(BF16))
    feat = total[0:128] + gown_ref[0:128, :]
    pos = total[128:136] + total[136:144] + gown_ref[128:136, :]
    for j in range(QUART):
        span = slice(128 * j, 128 * j + 128)
        part[j, 0:128, :] = feat[:, span]
        part[j, 128:136, :] = pos[:, span]

    sums = []
    for j in range(1, QUART):
        peer = lax.rem(quarter + j, QUART)
        copy = pltpu.make_async_remote_copy(
            src_ref=part.at[peer],
            dst_ref=heard.at[j - 1],
            send_sem=back_send_sem.at[PAIRS + j - 1],
            recv_sem=back_recv_sem.at[PAIRS + j - 1],
            device_id=(me, peer),
            device_id_type=MESH,
        )
        copy.start()
        sums.append(copy)
    got = part[quarter]
    for j, copy in enumerate(sums):
        copy.wait_recv()
        got = got + heard[j]
    grad_ref[...] = got
    for copy in backs + sums + [pool]:
        copy.wait_send()


def finish_kernel(energy_ref, grad_ref, wup_ref, energy_out, force_out, fgrad_out):
    energy_out[...] = energy_ref[...]
    force_out[...] = -grad_ref[128:131, :]
    fgrad_out[...] = lax.dot_general(
        grad_ref[0:128, :].T,
        wup_ref[...].astype(F32),
        (((1,), (1,)), ((), ())),
        precision=HIGH,
        preferred_element_type=F32,
    )


def interaction_call(dom_size, *operands):
    sds = jax.ShapeDtypeStruct
    edge_total = OWN * RANKS
    return pl.pallas_call(
        lambda *refs: interaction_kernel(dom_size, *refs),
        out_shape=(sds((1, OWN), F32), sds((136, OWN), F32)),
        in_specs=[VMEM_SPEC] * 6 + [pl.BlockSpec(memory_space=pltpu.SMEM)] + [VMEM_SPEC] * 6,
        out_specs=(VMEM_SPEC,) * 2,
        scratch_shapes=[
            pltpu.VMEM((RANKS, OWN), I32),
            pltpu.VMEM((2, PAIRS, BLK, 128), BF16),
            pltpu.VMEM((CH, ATOMS), BF16),
            pltpu.VMEM((2, PAIRS, BLK, 128), BF16),
            pltpu.VMEM((136, ATOMS), F32),
            pltpu.VMEM((PAIRS, BLK, 128), BF16),
            pltpu.VMEM((QUART, EDGE_ROWS, 128), I32),
            pltpu.VMEM((256, 384), BF16),
            pltpu.VMEM((TROWS, 256), BF16),
            pltpu.VMEM((TROWS, 256), F32),
            pltpu.VMEM((GROWS, edge_total), BF16),
            pltpu.VMEM((256, edge_total), BF16),
            pltpu.VMEM((9 * CH, OWN), F32),
            pltpu.VMEM((3 * CH, edge_total), F32),
            pltpu.VMEM((CH, edge_total), F32),
            pltpu.VMEM((64, edge_total), F32),
            pltpu.VMEM((64, edge_total), F32),
            pltpu.VMEM((8, edge_total), F32),
            pltpu.VMEM((8, edge_total), F32),
            pltpu.VMEM((GROUPS * GROWS, 256), F32),
            pltpu.VMEM((128, 128), F32),
            pltpu.VMEM((64, 24), BF16),
            pltpu.VMEM((64, 192), BF16),
            pltpu.VMEM((384, 192), BF16),
            pltpu.VMEM((8, 192), BF16),
            pltpu.VMEM((64, 192), BF16),
            pltpu.VMEM((128, 384), BF16),
            pltpu.VMEM((24, NE), F32),
            pltpu.VMEM((128, 5 * CH), F32),
            pltpu.VMEM((128, OWN), F32),
            pltpu.VMEM((PAIRS, BLK, 128), BF16),
            pltpu.VMEM((PAIRS, BLK, 128), BF16),
            pltpu.VMEM((PAIRS, BLK, 128), BF16),
            pltpu.VMEM((QUART, 136, 128), F32),
            pltpu.VMEM((QUART - 1, 136, 128), F32),
            pltpu.SemaphoreType.DMA((PAIRS + QUART,)),
            pltpu.SemaphoreType.DMA((PAIRS + QUART,)),
            pltpu.SemaphoreType.DMA((PAIRS + QUART,)),
            pltpu.SemaphoreType.DMA((PAIRS + QUART,)),
        ],
        compiler_params=pltpu.CompilerParams(
            collective_id=0, has_side_effects=True, vmem_limit_bytes=LIMIT
        ),
        name="interaction",
    )(*operands)


def on_device(
    dom_size, coordinates, features, species, ghost_map, edge_sender, edge_receiver, edge_count,
    w_up, radial_one, radial_two, radial_three, read_mix, species_out,
):
    sds = jax.ShapeDtypeStruct
    energy, grad = interaction_call(
        dom_size, features, w_up, coordinates, ghost_map,
        edge_sender.reshape(EDGE_ROWS, 128), edge_receiver.reshape(EDGE_ROWS, 128), edge_count,
        species.reshape(QUART, OWN), radial_one, radial_two, radial_three, read_mix, species_out,
    )
    energy, forces, feature_grad = pl.pallas_call(
        finish_kernel,
        out_shape=(sds((1, OWN), F32), sds((3, OWN), F32), sds((OWN, CH), F32)),
        in_specs=[VMEM_SPEC] * 3,
        out_specs=(VMEM_SPEC,) * 3,
        name="finish",
    )(energy, grad, w_up)
    return energy.reshape(OWN), forces, feature_grad


def solution(mesh):
    dom_size = mesh.shape["dom"]
    return jax.shard_map(
        lambda *args: on_device(dom_size, *args),
        mesh=mesh,
        in_specs=(
            P(None, "dom"),
            P("dom", None),
            P("dom"),
            P("dom", None),
            P(("dom", "edge")),
            P(("dom", "edge")),
            P("dom"),
            P(),
            P(),
            P(),
            P(),
            P(),
            P(),
        ),
        out_specs=(P(("dom", "edge")), P(None, ("dom", "edge")), P(("dom", "edge"), None)),
        check_vma=False,
    )
```

```python
import jax
import jax.numpy as jnp
from jax import lax
from jax.experimental import pallas as pl
from jax.experimental.pallas import tpu as pltpu
from jax.sharding import PartitionSpec as P

F32, BF16, I32 = jnp.float32, jnp.bfloat16, jnp.int32
HIGH = lax.Precision.HIGHEST
MESH = pl.DeviceIdType.MESH
VMEM_SPEC = pl.BlockSpec(memory_space=pltpu.VMEM)

CH = 128
ATOMS = 512
OWN = 128
RANKS = 64
SLOT = 64
NOFF = 26
PAIRS = NOFF // 2
QUART = 4
EDGE_ROWS = 64
GROUPS = 9
GROWS = 144
TROWS = 1232
PER = 16
NE = PER * OWN
STEPS = OWN * RANKS // NE
SORT_ROWS = 64
BLK = 80
SENTINEL = 4095
PARTS = ([7, 8], [5, 6], [3, 4], [2])
LIMIT = 56 * 1024 * 1024

OFFSETS = [
    (a, b, c)
    for a in (-1, 0, 1)
    for b in (-1, 0, 1)
    for c in (-1, 0, 1)
    if (a, b, c) != (0, 0, 0)
]


SEND_ORDER = sorted(range(PAIRS), key=lambda i: -abs(2 * i - PAIRS + 1))


def shifts(count):
    side = 1
    while side * side * side < count:
        side += 1
    return [o[0] * side * side + o[1] * side + o[2] for o in OFFSETS]


def mm(a, b):
    return lax.dot_general(a, b, (((1,), (0,)), ((), ())), preferred_element_type=F32)


def mm_nt(a, b):
    return lax.dot_general(a, b, (((1,), (1,)), ((), ())), preferred_element_type=F32)


def mm_high(a, b):
    return lax.dot_general(
        a, b, (((1,), (0,)), ((), ())), precision=HIGH, preferred_element_type=F32
    )


def split(x):
    hi = x.astype(BF16)
    return hi, (x - hi.astype(F32)).astype(BF16)


def weight_stack(w):
    hi, lo = split(w)
    return jnp.concatenate([hi, hi, lo], axis=1)


def value_stack(x):
    hi, lo = split(x)
    return jnp.concatenate([hi, lo, hi], axis=0)


def iota(shape, dim):
    return lax.broadcasted_iota(I32, shape, dim)


def fold(x):
    parts = [x[:, 128 * j : 128 * (j + 1)] for j in range(x.shape[1] // 128)]
    while len(parts) > 1:
        parts = [parts[j] + parts[j + 1] for j in range(0, len(parts), 2)]
    return parts[0]


def map_rows(gmap_ref, core, i):
    other = min(i + 1, PAIRS - 1)
    return jnp.concatenate(
        [gmap_ref[pl.ds(2 * i + core, 1), :], gmap_ref[pl.ds(2 * other + core, 1), :]], axis=1
    )


def offset_device(dom_size, i, core, sign):
    me, quarter = lax.axis_index("dom"), lax.axis_index("edge")
    even, odd = [(shifts(dom_size)[2 * i + j] * sign) % dom_size for j in (0, 1)]
    swap_even, swap_odd = [int(OFFSETS[2 * i + j][2] != 0) for j in (0, 1)]
    there = lax.rem(me + even + core * (odd - even), dom_size)
    swap = swap_even + core * (swap_odd - swap_even)
    return there, lax.rem(quarter + 2 * swap, QUART)


def greet(dom_size):
    barrier = pltpu.get_barrier_semaphore()
    quarter = lax.axis_index("edge")
    me = lax.axis_index("dom")
    core = lax.rem(quarter, 2)
    for i in range(PAIRS):
        for sign in (1, -1):
            there = offset_device(dom_size, i, core, sign)
            pl.semaphore_signal(barrier, inc=1, device_id=there, device_id_type=MESH)
    for j in range(1, QUART):
        peer = lax.rem(quarter + j, QUART)
        pl.semaphore_signal(barrier, inc=1, device_id=(me, peer), device_id_type=MESH)
    return barrier


def landed_block(copies, landed, i):
    copies[i].wait_recv()
    return landed[i].astype(F32)


def interaction_kernel(
    dom_size,
    feat_ref, wup_ref, coord_ref, gmap_ref, snd_ref, rcv_ref, cnt_ref, species_ref,
    w1_ref, w2_ref, w3_ref, mix_ref, sp_ref,
    energy_ref, grad_ref,
    slots_ref, blocks_ref, own_ref, gblocks_ref, gown_ref,
    sendblk, epack, tri_s,
    tab, tab32, dh_s, hot_s, acc, rad_s, h_s, d1_s, d2_s, bas_s, row_s, scat, sp_s,
    w1f, w2f, w3f, w1b, w2b, w3b, myc, mix_t, kind_s,
    matebuf, backblk, landed, sums_s, heard, send_sem, recv_sem, back_send_sem, back_recv_sem,
):
    me = lax.axis_index("dom")
    quarter = lax.axis_index("edge")
    core = lax.rem(quarter, 2)
    mate = quarter + 1 - 2 * core
    barrier = greet(dom_size)

    first = quarter * (EDGE_ROWS * 128)
    index = first + iota((EDGE_ROWS, 128), 0) * 128 + iota((EDGE_ROWS, 128), 1)
    sender = jnp.where(index < cnt_ref[0], snd_ref[...], SENTINEL)
    epack[quarter] = sender + rcv_ref[...] * 65536

    hprime = mm(feat_ref[...], wup_ref[...]).astype(BF16)
    h_t = hprime.astype(F32).T.astype(BF16)
    own_ref[...] = h_t
    coords = jnp.concatenate(
        [coord_ref[...].astype(F32), jnp.zeros((13, ATOMS), F32)], axis=0
    ).astype(BF16)
    ext = jnp.concatenate([h_t, coords], axis=0)

    low = iota((64, 128), 1) < 64
    low16 = iota((16, 128), 1) < 64
    low8 = iota((8, 128), 1) < 64
    sub8 = iota((8, 128), 0)
    for i in range(0, PAIRS, 2):
        onehot = jnp.where(iota((ATOMS, 128), 0) == map_rows(gmap_ref, core, i), 1.0, 0.0)
        picked = mm(ext, onehot.astype(BF16))
        top, bottom, pos = picked[0:64], picked[64:128], picked[128:144]
        sendblk[i, 0:64, :] = jnp.where(low, top, pltpu.roll(bottom, 64, 1)).astype(BF16)
        sendblk[i, 64:80, :] = pos.astype(BF16)
        if i + 1 < PAIRS:
            sendblk[i + 1, 0:64, :] = jnp.where(low, pltpu.roll(top, 64, 1), bottom).astype(BF16)
            sendblk[i + 1, 64:80, :] = pltpu.roll(pos, 64, 1).astype(BF16)

    pl.semaphore_wait(barrier, NOFF + QUART - 1)

    copies = []
    for j in range(1, QUART):
        peer = lax.rem(quarter + j, QUART)
        copy = pltpu.make_async_remote_copy(
            src_ref=epack.at[quarter],
            dst_ref=epack.at[quarter],
            send_sem=send_sem.at[PAIRS + j - 1],
            recv_sem=recv_sem.at[PAIRS + j - 1],
            device_id=(me, peer),
            device_id_type=MESH,
        )
        copy.start()
        copies.append(copy)

    ghosts = [None] * PAIRS
    for j in SEND_ORDER:
        copy = pltpu.make_async_remote_copy(
            src_ref=sendblk.at[j],
            dst_ref=blocks_ref.at[core, j],
            send_sem=send_sem.at[j],
            recv_sem=recv_sem.at[j],
            device_id=offset_device(dom_size, j, core, 1),
            device_id_type=MESH,
        )
        copy.start()
        ghosts[j] = copy

    coords = coord_ref[...].astype(F32)
    coords8 = jnp.concatenate([coords, jnp.zeros((5, ATOMS), F32)], axis=0)
    def place(g, lanes, rows):
        for t in range(17):
            tab32[8 * (GROUPS * t + g) : 8 * (GROUPS * t + g) + 8, lanes] = rows[8 * t : 8 * t + 8]

    for g in range(2):
        span = slice(256 * g, 256 * g + 256)
        place(g, slice(0, 256), jnp.concatenate([own_ref[:, span].astype(F32), coords8[:, span]], axis=0))
    place(8, slice(0, 256), jnp.zeros((136, 256), F32))
    tab32[8 * GROUPS * 17 :, :] = jnp.zeros((TROWS - 8 * GROUPS * 17, 256), F32)
    w1f[...] = weight_stack(w1_ref[...].T)
    w2f[...] = weight_stack(w2_ref[...].T)
    w3f[...] = weight_stack(w3_ref[...].T)
    w1b[...] = weight_stack(w1_ref[...])
    w2b[...] = weight_stack(w2_ref[...])
    hi, lo = split(w3_ref[...])
    w3b[...] = jnp.concatenate([hi, lo], axis=0)

    acc[...] = jnp.zeros(acc.shape, F32)
    scat[...] = jnp.zeros(scat.shape, F32)
    mine = pl.ds(pl.multiple_of(quarter * OWN, OWN), OWN)
    my_coords = coord_ref[:, mine].astype(F32)
    for c in range(3):
        mc = jnp.broadcast_to(my_coords[c : c + 1], (8, 128))
        myc[8 * c : 8 * c + 8, :] = jnp.concatenate([mc] * PER, axis=1)

    beta = jnp.zeros((8, NE), F32)
    for n in range(8):
        beta = jnp.where(iota((8, NE), 0) == n, 0.4 * 15.0 ** (n / 7.0), beta)

    sp_s[...] = jnp.zeros((128, 128), F32)
    sp_s[0:89, :] = sp_ref[...]
    kinds = species_ref[pl.ds(quarter, 1), :]
    kind_hot = jnp.where(iota((128, 128), 0) == kinds, 1.0, 0.0)
    kind_s[...] = mm_high(sp_s[...].T, kind_hot)
    mix_t[...] = mix_ref[...].T

    tri_s[:, 0:256] = jnp.where(iota((256, 256), 0) < iota((256, 256), 1), 1.0, 0.0).astype(BF16)
    tri_s[:, 256:384] = jnp.ones((256, 128), BF16)

    atom = iota((OWN, 256), 0).astype(F32)
    rank_of = iota((RANKS, 256), 0).astype(F32)

    share = pltpu.make_async_remote_copy(
        src_ref=blocks_ref.at[core],
        dst_ref=blocks_ref.at[core],
        send_sem=send_sem.at[PAIRS + QUART - 1],
        recv_sem=recv_sem.at[PAIRS + QUART - 1],
        device_id=(me, mate),
        device_id_type=MESH,
    )

    def sort_step(step, carry):
        base, total = carry
        for j in range(1, QUART):

            @pl.when(step == j)
            def _():
                copies[j - 1].wait_recv()

        @pl.when(step == QUART - 1)
        def _():
            for copy in ghosts:
                copy.wait_recv()
            share.start()

        packed = epack[lax.rem(quarter + QUART - step, QUART)]
        local = (packed >> 16) - quarter * OWN
        inside = (local >= 0) & (local < OWN)
        li8 = jnp.where(inside, local, 255).astype(F32)
        value = packed & 65535
        g8 = (value >> 8).astype(F32)
        hi8 = (value & 255).astype(F32)

        def lane_row(x, b):
            return jnp.concatenate([x[2 * b : 2 * b + 1], x[2 * b + 1 : 2 * b + 2]], axis=1)

        hots = [jnp.where(atom == lane_row(li8, b), 1.0, 0.0) for b in range(SORT_ROWS // 2)]
        hots16 = [hot.astype(BF16) for hot in hots]
        counts = mm(jnp.concatenate(hots16, axis=0), tri_s[...])
        lefts = []
        for b in range(SORT_ROWS // 2):
            block = counts[OWN * b : OWN * (b + 1)]
            before = block[:, 0:256] + jnp.concatenate([base, base], axis=1)
            base = base + block[:, 256:384]
            rank = jnp.sum(before * hots[b], axis=0, keepdims=True)
            here = rank_of == rank
            lefts.append(
                jnp.concatenate(
                    [
                        jnp.where(here, lane_row(g8, b), 0.0).astype(BF16),
                        jnp.where(here, lane_row(hi8, b), 0.0).astype(BF16),
                    ],
                    axis=0,
                )
            )
        total = total + mm_nt(jnp.concatenate(lefts, axis=1), jnp.concatenate(hots16, axis=1))
        return base, total

    zero = jnp.zeros((OWN, 128), F32)
    _, total = lax.fori_loop(0, QUART * EDGE_ROWS // SORT_ROWS, sort_step, (zero, zero))
    slots_ref[...] = (total[0:64] * 256.0 + total[64:128]).astype(I32)
    share.wait_recv()
    for copy in copies + ghosts + [share]:
        copy.wait_send()


    for p in range(PAIRS):
        g, at = 2 + p // 2, 128 * (p % 2)
        even = blocks_ref[0, p].astype(F32)
        odd = blocks_ref[1, p].astype(F32)
        top = jnp.where(low, even[0:64], pltpu.roll(odd[0:64], 64, 1))
        bottom = jnp.where(low, pltpu.roll(even[0:64], 64, 1), odd[0:64])
        pos = jnp.where(low8, even[64:72], pltpu.roll(odd[64:72], 64, 1))
        oe, oo = OFFSETS[2 * p], OFFSETS[2 * p + 1]
        for c in range(3):
            if oe[c] != 0 or oo[c] != 0:
                pos = jnp.where(sub8 == 3 + c, jnp.where(low8, float(oe[c]), float(oo[c])), pos)
        place(g, slice(at, at + 128), jnp.concatenate([top, bottom, pos], axis=0))
    tab[...] = tab32[...].astype(BF16)

    def slot_row(step):
        s = jnp.concatenate(
            [slots_ref[pl.ds(PER * step + j, 1), :] for j in range(PER)], axis=1
        )
        return jnp.broadcast_to(s, (8, NE))

    def harmonic(x, y, z, dsq):
        third = dsq * (1.0 / 3.0)
        return [None, x, y, z, x * y, y * z, x * z, x * x - third, y * y - third]

    degree = [0, 1, 1, 1, 2, 2, 2, 2, 2]

    def act(pre):
        sig = 0.5 + 0.5 * jnp.tanh(0.5 * pre)
        out = pre * sig
        return out, sig + out * (1.0 - sig)

    def gather(step, lanes, _):
        s = slot_row(step)
        group = s >> 8
        hi = s & 255
        valid = jnp.where(group < GROUPS, 1.0, 0.0)
        sub = iota((8, NE), 0)
        onehot = jnp.concatenate(
            [jnp.where(sub + 8 * t == hi, 1.0, 0.0) for t in range(32)], axis=0
        ).astype(BF16)
        hot_s[:, lanes] = onehot
        got = mm(tab[...], onehot)
        masks = [group == k for k in range(GROUPS)]
        for t in range(17):
            v = jnp.zeros((8, NE), F32)
            for k in range(GROUPS):
                at = 8 * (GROUPS * t + k)
                v = jnp.where(masks[k], got[at : at + 8], v)
            if t < 16:
                h_s[8 * t : 8 * t + 8, lanes] = v
        return v, valid

    def radial_one(step, lanes, given):
        pos, valid = given
        sub = iota((8, NE), 0)
        rel = []
        for c in range(3):
            sent = pos[c : c + 1] - pos[3 + c : 4 + c]
            rel.append(jnp.broadcast_to(sent, (8, NE)) - myc[8 * c : 8 * c + 8, :])
        x, y, z = rel
        dsq = x * x + y * y + z * z
        e0 = jnp.maximum(0.0, 1.0 - dsq * 0.25) * valid
        basis = jnp.exp(-dsq * beta)
        packed = jnp.zeros((8, NE), F32)
        for j, v in enumerate((x, y, z, dsq, e0 * e0, e0)):
            packed = jnp.where(sub == j, v, packed)
        row_s[:, lanes] = packed
        bas_s[:, lanes] = basis
        return mm(w1f[...], value_stack(basis))

    def radial_two(step, lanes, pre):
        h1, d1 = act(pre)
        d1_s[:, lanes] = d1
        return mm(w2f[...], value_stack(h1))

    def radial_three(step, lanes, pre):
        h2, d2 = act(pre)
        d2_s[:, lanes] = d2
        rad_s[:, lanes] = mm(w3f[...], value_stack(h2))

    def row_values(lanes):
        rows = row_s[:, lanes]
        return [jnp.broadcast_to(rows[j : j + 1], (8, NE)) for j in range(6)]

    def gather_sums(step, lanes, _):
        x, y, z, dsq, env, _ = row_values(lanes)
        ys = harmonic(x, y, z, dsq)
        for t in range(16):
            he = h_s[8 * t : 8 * t + 8, lanes] * env
            ds = [he * rad_s[128 * l + 8 * t : 128 * l + 8 * t + 8, lanes] for l in range(3)]
            for m in range(9):
                msg = ds[degree[m]] if m == 0 else ds[degree[m]] * ys[m]
                at = 128 * m + 8 * t
                acc[at : at + 8, :] += fold(msg)

    def staged(stages, step):
        lanes = pl.ds(pl.multiple_of(step * NE, NE), NE)
        held = None
        for stage in stages:
            held = stage(step, lanes, held)
        return held

    def fwd(step, carry):
        staged([gather, radial_one, radial_two, radial_three, gather_sums], step)
        return carry

    lax.fori_loop(0, STEPS, fwd, 0)

    def node(m):
        return acc[128 * m : 128 * m + 128, :] * 0.125

    a0, vx, vy, vz, xy, yz, xz, xx, yy = [node(m) for m in range(9)]
    zz = -xx - yy
    n1 = vx * vx + vy * vy + vz * vz
    n2 = xx * xx + yy * yy + zz * zz + 2.0 * (xy * xy + yz * yz + xz * xz)
    cx = xx * vx + xy * vy + xz * vz
    cy = xy * vx + yy * vy + yz * vz
    cz = xz * vx + yz * vy + zz * vz
    cub = cx * vx + cy * vy + cz * vz
    inv = jnp.concatenate([a0, n1, n2, a0 * n1, cub], axis=0)
    pre = mm_high(mix_t[...], inv)
    sig = 0.5 + 0.5 * jnp.tanh(0.5 * pre)
    hid = pre * sig
    per_kind = kind_s[...]
    energy_ref[...] = jnp.sum(hid * per_kind, axis=0, keepdims=True)
    dpre = per_kind * (sig + hid * (1.0 - sig))
    dinv = mm_high(mix_ref[...], dpre) * 0.125
    g0, g1, g2, g3, g4 = [dinv[128 * j : 128 * j + 128] for j in range(5)]
    w = 2.0 * (g1 + g3 * a0)
    c2 = 2.0 * g4
    acc[0:128, :] = g0 + g3 * n1
    acc[128:256, :] = w * vx + c2 * cx
    acc[256:384, :] = w * vy + c2 * cy
    acc[384:512, :] = w * vz + c2 * cz
    acc[512:640, :] = 4.0 * xy * g2 + c2 * vx * vy
    acc[640:768, :] = 4.0 * yz * g2 + c2 * vy * vz
    acc[768:896, :] = 4.0 * xz * g2 + c2 * vx * vz
    acc[896:1024, :] = 2.0 * g2 * (xx - zz) + g4 * (vx * vx - vz * vz)
    acc[1024:1152, :] = 2.0 * g2 * (yy - zz) + g4 * (vy * vy - vz * vz)

    def grads_part(lanes, part, state):
        x, y, z, dsq, env, _ = row_values(lanes)
        ys = harmonic(x, y, z, dsq)
        denv, dys, drs = state
        dhs = []
        for t in range(4 * part, 4 * part + 4):
            da = []
            for m in range(9):
                v = acc[128 * m + 8 * t : 128 * m + 8 * t + 8, :]
                da.append(jnp.concatenate([v] * PER, axis=1))
            t0 = da[0]
            t1 = x * da[1] + y * da[2] + z * da[3]
            t2 = ys[4] * da[4]
            for m in range(5, 9):
                t2 = t2 + ys[m] * da[m]
            ts = [t0, t1, t2]
            rs = [rad_s[128 * l + 8 * t : 128 * l + 8 * t + 8, lanes] for l in range(3)]
            u = rs[0] * t0 + rs[1] * t1 + rs[2] * t2
            h = h_s[8 * t : 8 * t + 8, lanes]
            he = h * env
            denv = denv + h * u
            dhs.append(env * u)
            for l in range(3):
                drs[l].append(he * ts[l])
            d1, d2 = he * rs[1], he * rs[2]
            for m in range(1, 9):
                dys[m] = dys[m] + (d1 if m < 4 else d2) * da[m]
        dh_s[32 * part : 32 * part + 32, lanes] = jnp.concatenate(dhs, axis=0).astype(BF16)
        return denv, dys, drs

    def radial_back_two(step, lanes, given):
        denv, dys, both = given
        dp2 = (both[0:64] + both[64:128]) * d2_s[:, lanes]
        return denv, dys, mm(w2b[...], value_stack(dp2))

    def radial_back_one(step, lanes, given):
        denv, dys, dh1 = given
        return denv, dys, mm(w1b[...], value_stack(dh1 * d1_s[:, lanes]))

    def position_grads(step, lanes, given):
        denv, dys, dbas = given

        def total(v):
            return jnp.broadcast_to(jnp.sum(v, axis=0, keepdims=True), (8, NE))

        x, y, z, _, _, e0 = row_values(lanes)
        denv = total(denv)
        dys = [None] + [total(v) for v in dys[1:]]
        ddsq = (
            -total(dbas * bas_s[:, lanes] * beta)
            - 0.5 * e0 * denv
            - (dys[7] + dys[8]) * (1.0 / 3.0)
        )
        two = 2.0 * ddsq
        dx = dys[1] + y * dys[4] + z * dys[6] + 2.0 * x * dys[7] + x * two
        dy = dys[2] + x * dys[4] + z * dys[5] + 2.0 * y * dys[8] + y * two
        dz = dys[3] + y * dys[5] + x * dys[6] + z * two
        sub = iota((8, NE), 0)
        return jnp.where(sub == 0, dx, jnp.where(sub == 1, dy, jnp.where(sub == 2, dz, 0.0)))

    def masked(step, lanes, groups):
        group = slot_row(step) >> 8
        group16 = jnp.concatenate([group, group], axis=0)
        lefts = []
        for k in groups:
            mask = jnp.where(group16 == k, 1.0, 0.0).astype(BF16)
            lefts.extend(dh_s[16 * t : 16 * t + 16, lanes] * mask for t in range(GROWS // 16))
        return jnp.concatenate(lefts, axis=0)

    def spread_part(step, lanes, groups):
        span = slice(GROWS * groups[0], GROWS * groups[-1] + GROWS)
        scat[span, :] += mm_nt(masked(step, lanes, groups), hot_s[:, lanes])

    down = jnp.zeros((8, 128), F32)
    for step in range(STEPS + 1):
        ahead = step < STEPS
        if ahead:
            lanes = slice(step * NE, step * NE + NE)
            state = jnp.zeros((8, NE), F32), [jnp.zeros((8, NE), F32) for _ in range(9)], [[], [], []]
        for part in range(4):
            if step > 0:
                spread_part(step - 1, slice(step * NE - NE, step * NE), PARTS[part])
            if ahead:
                state = grads_part(lanes, part, state)
        if ahead:
            denv, dys, drs = state
            drad = jnp.concatenate(drs[0] + drs[1] + drs[2], axis=0).astype(BF16)
            given = radial_back_two(step, lanes, (denv, dys, mm(w3b[...], drad)))
            given = radial_back_one(step, lanes, given)
            drel = position_grads(step, lanes, given)
            drel_hi = drel.astype(BF16).astype(F32)
            dh_s[128:144, lanes] = jnp.concatenate([drel_hi, drel - drel_hi], axis=0).astype(BF16)
            down = down + fold(drel)

    for p in range(PAIRS):
        g, at = 2 + p // 2, 128 * (p % 2)
        top = scat[GROWS * g : GROWS * g + 64, at : at + 128]
        bottom = scat[GROWS * g + 64 : GROWS * g + 128, at : at + 128]
        pos = (
            scat[GROWS * g + 128 : GROWS * g + 136, at : at + 128]
            + scat[GROWS * g + 136 : GROWS * g + 144, at : at + 128]
        )
        pos_hi = pos.astype(BF16).astype(F32)
        pos = jnp.concatenate([pos_hi, pos - pos_hi], axis=0)
        even = jnp.where(low, top, pltpu.roll(bottom, 64, 1))
        odd = jnp.where(low, pltpu.roll(top, 64, 1), bottom)
        gblocks_ref[0, p, 0:64, :] = even.astype(BF16)
        gblocks_ref[1, p, 0:64, :] = odd.astype(BF16)
        gblocks_ref[0, p, 64:80, :] = jnp.where(low16, pos, 0.0).astype(BF16)
        gblocks_ref[1, p, 64:80, :] = jnp.where(low16, pltpu.roll(pos, 64, 1), 0.0).astype(BF16)


    pool = pltpu.make_async_remote_copy(
        src_ref=gblocks_ref.at[1 - core],
        dst_ref=matebuf,
        send_sem=back_send_sem.at[PAIRS + QUART - 1],
        recv_sem=back_recv_sem.at[PAIRS + QUART - 1],
        device_id=(me, mate),
        device_id_type=MESH,
    )
    pool.start()

    def own_spread(step, carry):
        lanes = pl.ds(pl.multiple_of(step * NE, NE), NE)
        scat[0 : 2 * GROWS, :] += mm_nt(masked(step, lanes, range(2)), hot_s[:, lanes])
        return carry

    lax.fori_loop(0, STEPS // 2, own_spread, 0)
    pool.wait_recv()
    backs = [None] * PAIRS
    for i in SEND_ORDER:
        backblk[i] = (gblocks_ref[core, i].astype(F32) + matebuf[i].astype(F32)).astype(BF16)
        copy = pltpu.make_async_remote_copy(
            src_ref=backblk.at[i],
            dst_ref=landed.at[i],
            send_sem=back_send_sem.at[i],
            recv_sem=back_recv_sem.at[i],
            device_id=offset_device(dom_size, i, core, -1),
            device_id_type=MESH,
        )
        copy.start()
        backs[i] = copy

    lax.fori_loop(STEPS // 2, STEPS, own_spread, 0)
    for g in range(2):
        span = slice(256 * g, 256 * g + 256)
        gown_ref[0:128, span] = scat[GROWS * g : GROWS * g + 128, :]
        gown_ref[128:136, span] = (
            scat[GROWS * g + 128 : GROWS * g + 136, :] + scat[GROWS * g + 136 : GROWS * g + 144, :]
        )
    gown_ref[128:136, mine] = gown_ref[128:136, mine] - down

    total = jnp.zeros((GROWS, ATOMS), F32)
    for i in range(0, PAIRS, 2):
        even = landed_block(backs, landed, i)
        odd = landed_block(backs, landed, i + 1) if i + 1 < PAIRS else jnp.zeros((BLK, 128), F32)
        top = jnp.where(low, even[0:64], pltpu.roll(odd[0:64], 64, 1))
        bottom = jnp.where(low, pltpu.roll(even[0:64], 64, 1), odd[0:64])
        pos = jnp.where(low16, even[64:80], pltpu.roll(odd[64:80], 64, 1))
        left = jnp.concatenate([top, bottom, pos], axis=0).astype(BF16)
        onehot = jnp.where(iota((ATOMS, 128), 0) == map_rows(gmap_ref, core, i), 1.0, 0.0)
        total = total + mm_nt(left, onehot.astype(BF16))
    feat = total[0:128] + gown_ref[0:128, :]
    pos = total[128:136] + total[136:144] + gown_ref[128:136, :]
    for j in range(QUART):
        span = slice(128 * j, 128 * j + 128)
        sums_s[j, 0:128, :] = feat[:, span]
        sums_s[j, 128:136, :] = pos[:, span]

    sums = []
    for j in range(1, QUART):
        peer = lax.rem(quarter + j, QUART)
        copy = pltpu.make_async_remote_copy(
            src_ref=sums_s.at[peer],
            dst_ref=heard.at[j - 1],
            send_sem=back_send_sem.at[PAIRS + j - 1],
            recv_sem=back_recv_sem.at[PAIRS + j - 1],
            device_id=(me, peer),
            device_id_type=MESH,
        )
        copy.start()
        sums.append(copy)
    got = sums_s[quarter]
    for j, copy in enumerate(sums):
        copy.wait_recv()
        got = got + heard[j]
    grad_ref[...] = got
    for copy in backs + sums + [pool]:
        copy.wait_send()


def finish_kernel(energy_ref, grad_ref, wup_ref, energy_out, force_out, fgrad_out):
    energy_out[...] = energy_ref[...]
    force_out[...] = -grad_ref[128:131, :]
    fgrad_out[...] = lax.dot_general(
        grad_ref[0:128, :].T,
        wup_ref[...].astype(F32),
        (((1,), (1,)), ((), ())),
        precision=HIGH,
        preferred_element_type=F32,
    )


def interaction_call(dom_size, *operands):
    sds = jax.ShapeDtypeStruct
    edge_total = OWN * RANKS
    return pl.pallas_call(
        lambda *refs: interaction_kernel(dom_size, *refs),
        out_shape=(sds((1, OWN), F32), sds((136, OWN), F32)),
        in_specs=[VMEM_SPEC] * 6 + [pl.BlockSpec(memory_space=pltpu.SMEM)] + [VMEM_SPEC] * 6,
        out_specs=(VMEM_SPEC,) * 2,
        scratch_shapes=[
            pltpu.VMEM((RANKS, OWN), I32),
            pltpu.VMEM((2, PAIRS, BLK, 128), BF16),
            pltpu.VMEM((CH, ATOMS), BF16),
            pltpu.VMEM((2, PAIRS, BLK, 128), BF16),
            pltpu.VMEM((136, ATOMS), F32),
            pltpu.VMEM((PAIRS, BLK, 128), BF16),
            pltpu.VMEM((QUART, EDGE_ROWS, 128), I32),
            pltpu.VMEM((256, 384), BF16),
            pltpu.VMEM((TROWS, 256), BF16),
            pltpu.VMEM((TROWS, 256), F32),
            pltpu.VMEM((GROWS, edge_total), BF16),
            pltpu.VMEM((256, edge_total), BF16),
            pltpu.VMEM((9 * CH, OWN), F32),
            pltpu.VMEM((3 * CH, edge_total), F32),
            pltpu.VMEM((CH, edge_total), F32),
            pltpu.VMEM((64, edge_total), F32),
            pltpu.VMEM((64, edge_total), F32),
            pltpu.VMEM((8, edge_total), F32),
            pltpu.VMEM((8, edge_total), F32),
            pltpu.VMEM((GROUPS * GROWS, 256), F32),
            pltpu.VMEM((128, 128), F32),
            pltpu.VMEM((64, 24), BF16),
            pltpu.VMEM((64, 192), BF16),
            pltpu.VMEM((384, 192), BF16),
            pltpu.VMEM((8, 192), BF16),
            pltpu.VMEM((64, 192), BF16),
            pltpu.VMEM((128, 384), BF16),
            pltpu.VMEM((24, NE), F32),
            pltpu.VMEM((128, 5 * CH), F32),
            pltpu.VMEM((128, OWN), F32),
            pltpu.VMEM((PAIRS, BLK, 128), BF16),
            pltpu.VMEM((PAIRS, BLK, 128), BF16),
            pltpu.VMEM((PAIRS, BLK, 128), BF16),
            pltpu.VMEM((QUART, 136, 128), F32),
            pltpu.VMEM((QUART - 1, 136, 128), F32),
            pltpu.SemaphoreType.DMA((PAIRS + QUART,)),
            pltpu.SemaphoreType.DMA((PAIRS + QUART,)),
            pltpu.SemaphoreType.DMA((PAIRS + QUART,)),
            pltpu.SemaphoreType.DMA((PAIRS + QUART,)),
        ],
        compiler_params=pltpu.CompilerParams(
            collective_id=0, has_side_effects=True, vmem_limit_bytes=LIMIT
        ),
        name="interaction",
    )(*operands)


def on_device(
    dom_size, coordinates, features, species, ghost_map, edge_sender, edge_receiver, edge_count,
    w_up, radial_one, radial_two, radial_three, read_mix, species_out,
):
    sds = jax.ShapeDtypeStruct
    energy, grad = interaction_call(
        dom_size, features, w_up, coordinates, ghost_map,
        edge_sender.reshape(EDGE_ROWS, 128), edge_receiver.reshape(EDGE_ROWS, 128), edge_count,
        species.reshape(QUART, OWN), radial_one, radial_two, radial_three, read_mix, species_out,
    )
    energy, forces, feature_grad = pl.pallas_call(
        finish_kernel,
        out_shape=(sds((1, OWN), F32), sds((3, OWN), F32), sds((OWN, CH), F32)),
        in_specs=[VMEM_SPEC] * 3,
        out_specs=(VMEM_SPEC,) * 3,
        name="finish",
    )(energy, grad, w_up)
    return energy.reshape(OWN), forces, feature_grad


def solution(mesh):
    dom_size = mesh.shape["dom"]
    return jax.shard_map(
        lambda *args: on_device(dom_size, *args),
        mesh=mesh,
        in_specs=(
            P(None, "dom"),
            P("dom", None),
            P("dom"),
            P("dom", None),
            P(("dom", "edge")),
            P(("dom", "edge")),
            P("dom"),
            P(),
            P(),
            P(),
            P(),
            P(),
            P(),
        ),
        out_specs=(P(("dom", "edge")), P(None, ("dom", "edge")), P(("dom", "edge"), None)),
        check_vma=False,
    )
```
